256 devices in a mesh: dp: 16 (over y, x), owner: 16 (over z, core).
Axes of the slice: x: 4, y: 4, z: 8, core: 2. Of those that a mesh axis runs over, the one named last changes fastest.
Arguments:
- acts: bfloat16 [2, 4096, 6144], P(None, 'dp'), may hold values from -6 to 6
- grads_out: bfloat16 [2, 4096, 24576], P(None, 'dp', 'owner'), may hold values from -6 to 6
- weight_grad: bfloat16 [2, 24576, 6144], P(None, 'owner', 'dp'), may hold values from -6 to 6
Outputs:
- preconditioned: bfloat16 [2, 24576, 6144], P(None, 'owner', 'dp')
The draws below stay inside these ranges and needn't reach their ends.
All inputs are finite; a program needn't handle non-finite values. Where the reference program divides by a largest or mean magnitude, that divisor is 1e-20 or more.
Results may differ from the reference program's by a relative error of at most 0.0098.
Values may be sent and summed in bfloat16 or wider, within the bound.
No kernel may reach another device: no remote copies, remote signals or barrier semaphores. Data moves between devices by JAX's collectives and lax.ppermute only.
A program may use at most 128 MiB of HBM per device.

```python
import jax
import jax.numpy as jnp
from jax import lax

D = 6144
FF = 24576
BLK = 512
ITERS = 2
LAYERS = 2
TOKENS = 4096


def levels(key, shape, split, low, top_value):
    factor_of = 1.0
    for position, blocks in split:
        draws = jax.random.uniform(jax.random.fold_in(jax.random.fold_in(key, 6), position), (blocks,), jnp.float32, low / len(split), top_value / len(split))
        factor_of = factor_of * jnp.repeat(jnp.exp(draws), shape[position] // blocks).reshape((-1,) + (1,) * (len(shape) - 1 - position))
    return factor_of


def noise(key, dims, deviation, reach, split=(), held_as=jnp.bfloat16):
    entries = deviation * jax.random.normal(key, dims, jnp.float32)
    if split:
        entries = entries * levels(key, dims, split, -0.22, 0.18)
    return jnp.clip(entries, -reach, reach).astype(held_as)


def setup_inputs(seed: int = 0) -> dict:
    seeds = jax.random.split(jax.random.key(seed), 4)
    acts = noise(seeds[0], (LAYERS, TOKENS, D), 1.0, 6.0, ((1, 16),))
    grads_out = noise(seeds[1], (LAYERS, TOKENS, FF), 1.0, 6.0, ((1, 16), (2, 16)))
    weight_grad = noise(seeds[2], (LAYERS, FF, D), 1.0, 6.0, ((1, 16), (2, 16)))
    return dict(acts=acts, grads_out=grads_out, weight_grad=weight_grad)


damping = 0.1


def newton(factor):
    eye = jnp.eye(BLK, dtype=jnp.float32)
    matrix = factor + damping * eye
    alpha = 1.0 / jnp.max(jnp.sum(jnp.abs(matrix), axis=2), axis=1)
    low = lax.optimization_barrier(matrix.astype(jnp.bfloat16)).astype(jnp.float32)
    iterate = (alpha[:, None, None] * eye).astype(jnp.bfloat16)
    for step in range(ITERS):
        image = jnp.einsum("bij,bjk->bik", low, iterate.astype(jnp.float32), precision=lax.Precision.HIGHEST)
        residue = (2.0 * eye - image).astype(jnp.bfloat16)
        iterate = jnp.einsum("bij,bjk->bik", iterate.astype(jnp.float32), residue.astype(jnp.float32), precision=lax.Precision.HIGHEST).astype(jnp.bfloat16)
    return iterate


def covariance(rows, count):
    wide = rows.reshape(TOKENS, count, BLK).astype(jnp.float32)
    return jnp.einsum("tai,taj->aij", wide, wide, precision=lax.Precision.HIGHEST) / TOKENS


def reference(acts, grads_out, weight_grad):
    results = []
    for layer in range(LAYERS):
        inv_a = newton(covariance(acts[layer], D // BLK))
        inv_g = newton(covariance(grads_out[layer], FF // BLK))
        gradient = weight_grad[layer].reshape(FF // BLK, BLK, D).astype(jnp.float32)
        left = jnp.einsum("gij,gjc->gic", inv_g.astype(jnp.float32), gradient, precision=lax.Precision.HIGHEST)
        left = left.astype(jnp.bfloat16).reshape(FF, D // BLK, BLK).astype(jnp.float32)
        right = jnp.einsum("rab,abc->rac", left, inv_a.astype(jnp.float32), precision=lax.Precision.HIGHEST)
        results.append(right.astype(jnp.bfloat16).reshape(FF, D))
    return jnp.stack(results)
```

```python
import jax
import jax.numpy as jnp
from jax import lax
from jax.experimental import pallas as pl
from jax.experimental.pallas import tpu as pltpu
from jax.sharding import Mesh, PartitionSpec as P

BLK = 512
SUB = 128
damping = 0.1
TOKENS = 4096
F32 = jnp.float32
BF16 = jnp.bfloat16
VMEM = pltpu.VMEM

PAIRS = [(r, c) for r in range(4) for c in range(r, 4)]
LANES = 15 * SUB


def tn_dot(a, b):
    return lax.dot_general(a, b, (((0,), (0,)), ((), ())), preferred_element_type=F32)


def nn_dot(a, b):
    return lax.dot_general(a, b, (((1,), (0,)), ((), ())), preferred_element_type=F32)


def cov_kernel(pos, acts, grads, g0, g1, g2, g3, h0, h1, h2, h3, pack):
    x, y, part = pos[0], pos[1], pos[3]
    first = (g0, g1, g2, g3)
    second = (h0, h1, h2, h3)
    for layer in range(2):
        for b in range(3):
            rows = grads[layer, :, b * BLK:(b + 1) * BLK]
            top = tn_dot(rows[:, :256], rows).astype(BF16)
            low = tn_dot(rows[:, 256:], rows[:, 256:]).astype(BF16)
            for i, (r, c) in enumerate(PAIRS):
                s = 10 * b + i
                if r < 2:
                    piece = top[r * SUB:(r + 1) * SUB, c * SUB:(c + 1) * SUB]
                else:
                    piece = low[(r - 2) * SUB:(r - 1) * SUB, (c - 2) * SUB:(c - 1) * SUB]
                pack[layer, s // 15 * SUB:(s // 15 + 1) * SUB, s % 15 * SUB:(s % 15 + 1) * SUB] = piece
    for d in range(4):
        first[d][...] = pack[0, pl.ds(pl.multiple_of((x + d) % 4 * 64, 64), 64), :]
        second[d][0:64, :] = pack[1, pl.ds(pl.multiple_of((y + d) % 4 * 64, 64), 64), :]
    k = lax.broadcasted_iota(jnp.int32, (BLK, 64), 0)
    m = lax.broadcasted_iota(jnp.int32, (BLK, 64), 1)
    select = jnp.where(k == m // 16 * SUB + part * 16 + m % 16, 1.0, 0.0).astype(BF16)
    for d in range(4):
        start = (y + d) % 4 * (3 * BLK)
        for j in range(3):
            rows = acts[0, :, pl.ds(pl.multiple_of(start + j * BLK, BLK), BLK)]
            chosen = nn_dot(rows, select).astype(BF16)
            cov = tn_dot(chosen, rows).astype(BF16)
            for i, (r, c) in enumerate(PAIRS):
                s = 10 * j + i
                second[d][64 + s // 15 * 16:80 + s // 15 * 16, s % 15 * SUB:(s % 15 + 1) * SUB] = (
                    cov[r * 16:(r + 1) * 16, c * SUB:(c + 1) * SUB]
                )


def invert(packed_piece, full):
    for i, (r, c) in enumerate(PAIRS):
        piece = packed_piece(i).astype(F32)
        full[r * SUB:(r + 1) * SUB, c * SUB:(c + 1) * SUB] = piece
        if r != c:
            full[c * SUB:(c + 1) * SUB, r * SUB:(r + 1) * SUB] = piece.T
    ri = lax.broadcasted_iota(jnp.int32, (BLK, BLK), 0)
    ci = lax.broadcasted_iota(jnp.int32, (BLK, BLK), 1)
    diagonal = ri == ci
    matrix = full[...] + jnp.where(diagonal, damping, 0.0)
    two_eye = jnp.where(diagonal, 2.0, 0.0)
    sums = jnp.sum(jnp.abs(matrix), axis=0, keepdims=True)
    alpha = (1.0 / jnp.max(sums, axis=1, keepdims=True)).astype(BF16).astype(F32)
    low = matrix.astype(BF16)
    residue = (two_eye - low.astype(F32) * alpha).astype(BF16)
    iterate = (residue.astype(F32) * alpha).astype(BF16)
    image = nn_dot(low, iterate)
    residue = (two_eye - image).astype(BF16)
    return nn_dot(iterate, residue).astype(BF16)


def right_kernel(pos, mine, other, w_own, w_pair, w_mid, out, pack, full, diag):
    x, core = pos[0], pos[2]
    for z in range(8):
        layer, q = z // 4, z % 4
        at = pl.multiple_of(q * 32 + core * 16, 16)
        pack[layer, pl.ds(at, 16), :] = mine[z * 16:(z + 1) * 16, :]
        at = pl.multiple_of(q * 32 + (1 - core) * 16, 16)
        pack[layer, pl.ds(at, 16), :] = other[z * 16:(z + 1) * 16, :]
    base = x // 2 * BLK
    own = pl.multiple_of(x * 384 - base, SUB)
    pair = pl.multiple_of((x + 1 - 2 * (x % 2)) * 384 - base, SUB)
    mid = pl.multiple_of(jnp.where(x == 1, 768, 0), SUB)
    for layer in range(2):
        for b in range(2):
            at = b * BLK
            inverse = invert(
                lambda i: pack[layer, :, b * 1280 + i * SUB:b * 1280 + (i + 1) * SUB], full.at[layer, b]
            )
            diag[layer, at:at + BLK, at:at + BLK] = inverse
            diag[layer, at:at + BLK, BLK - at:2 * BLK - at] = jnp.zeros((BLK, BLK), BF16)
        columns = pl.ds(own, 384)
        total = nn_dot(w_own[layer], diag[layer, pl.ds(own, 384), columns])
        total += nn_dot(w_pair[layer], diag[layer, pl.ds(pair, 384), columns])
        total += nn_dot(w_mid[layer], diag[layer, pl.ds(mid, 256), columns])
        out[layer] = total.astype(BF16)


def left_kernel(pos, *refs):
    first, second, right, out, pack, full = refs[0:4], refs[4:8], refs[8], refs[9], refs[10], refs[11]
    x, y = pos[0], pos[1]
    for d in range(4):
        for e in range(4):
            at = (x + 4 - d) % 4 * 64 + (y + 4 - e) % 4 * 16
            pack[0, pl.ds(pl.multiple_of(at, 16), 16), :] = first[d][e * 16:(e + 1) * 16, :]
            at = (y + 4 - d) % 4 * 64 + (x + 4 - e) % 4 * 16
            pack[1, pl.ds(pl.multiple_of(at, 16), 16), :] = second[d][e * 16:(e + 1) * 16, :]
    for layer in range(2):
        for b in range(3):
            def piece(i):
                s = 10 * b + i
                return pack[layer, s // 15 * SUB:(s // 15 + 1) * SUB, s % 15 * SUB:(s % 15 + 1) * SUB]
            inverse = invert(piece, full.at[layer, b])
            at = b * BLK
            out[layer, at:at + BLK, :] = nn_dot(inverse, right[layer, at:at + BLK, :]).astype(BF16)


def call(kernel, pos, operands, in_specs, out_shape, scratch, flops):
    spec = pl.BlockSpec(memory_space=VMEM)
    return pl.pallas_call(
        kernel,
        grid_spec=pltpu.PrefetchScalarGridSpec(
            num_scalar_prefetch=1,
            grid=(1,),
            in_specs=in_specs,
            out_specs=[pl.BlockSpec(s.shape, lambda i, p, n=len(s.shape): (0,) * n) for s in out_shape],
            scratch_shapes=scratch,
        ),
        out_shape=out_shape,
        compiler_params=pltpu.CompilerParams(vmem_limit_bytes=48 * 1024 * 1024),
        cost_estimate=pl.CostEstimate(flops=flops, bytes_accessed=8_000_000, transcendentals=0),
    )(pos, *operands)


def whole(a):
    return pl.BlockSpec(a.shape, lambda i, p, n=a.ndim: (0,) * n)


def shift(a, axis, d):
    return lax.ppermute(a, axis, [(i, (i + d) % 4) for i in range(4)])


def add(parts):
    return sum(p.astype(F32) for p in parts)


def spread(parts, axis):
    return [parts[0]] + [shift(parts[d], axis, d) for d in (1, 2, 3)]


def gather(a, axis):
    return [a] + [shift(a, axis, d) for d in (1, 2, 3)]


def chunk(a, index, rows):
    return lax.dynamic_slice_in_dim(a, index % 4 * rows, rows, 0)


def body(acts, grads_out, weight_grad):
    y, x, z, c = (lax.axis_index(n) for n in ("y", "x", "z", "c"))
    part = z % 4 * 2 + c
    pos = jnp.stack([x, y, c, part, z // 4]).astype(jnp.int32)

    w_pair = lax.ppermute(weight_grad, "x", [(0, 1), (1, 0), (2, 3), (3, 2)])
    middle = lax.dynamic_slice_in_dim(weight_grad, jnp.where(x == 1, SUB, 0), 256, 2)
    w_mid = lax.ppermute(middle, "x", [(1, 2), (2, 1)])

    shapes = [jax.ShapeDtypeStruct((64, LANES), BF16)] * 4 + [jax.ShapeDtypeStruct((96, LANES), BF16)] * 4
    covs = call(
        cov_kernel, pos, (acts, grads_out),
        [pl.BlockSpec((1, 256, 6144), lambda i, p: (p[4], 0, 0)), whole(grads_out)],
        shapes, [VMEM((2, 256, LANES), BF16)], 3_000_000_000,
    )
    first = add(spread(covs[:4], "x")).astype(BF16)
    both = add(spread(covs[4:], "y")).astype(BF16)
    second, side = both[:64], both[64:]

    sends = [jnp.concatenate([chunk(second, x + d, 16), side], axis=0) for d in range(4)]
    both = add(spread(sends, "x")) * (1.0 / TOKENS)
    first = (add(spread([chunk(first, y + d, 16) for d in range(4)], "y")) * (1.0 / TOKENS)).astype(BF16)
    second = both[:16].astype(BF16)
    side = jnp.concatenate([both[16:32], both[32:48]], axis=1)
    side = lax.dynamic_slice_in_dim(side, x // 2 * 1280, 2560, 1).astype(BF16)

    sides = lax.all_to_all(jnp.tile(side, (8, 1)), "z", 0, 0, tiled=True)
    first = jnp.concatenate(gather(first, "y"), axis=0)
    second = jnp.concatenate(gather(second, "x"), axis=0)
    first = gather(first, "x")
    second = gather(second, "y")
    other = lax.ppermute(sides, "c", [(0, 1), (1, 0)])

    right = call(
        right_kernel, pos, (sides, other, weight_grad, w_pair, w_mid),
        [whole(a) for a in (sides, other, weight_grad, w_pair, w_mid)],
        [jax.ShapeDtypeStruct(weight_grad.shape, BF16)],
        [VMEM((2, 128, 2560), BF16), VMEM((2, 2, BLK, BLK), F32), VMEM((2, 1024, 1024), BF16)],
        5_000_000_000,
    )[0]
    operands = (*first, *second, right)
    return call(
        left_kernel, pos, operands, [whole(a) for a in operands],
        [jax.ShapeDtypeStruct(weight_grad.shape, BF16)],
        [VMEM((2, 256, LANES), BF16), VMEM((2, 3, BLK, BLK), F32)],
        5_000_000_000,
    )[0]


def solution(mesh):
    fine = Mesh(mesh.devices.reshape(4, 4, 8, 2), ("y", "x", "z", "c"))
    dp, owner = ("y", "x"), ("z", "c")
    in_specs = (P(None, dp, None), P(None, dp, owner), P(None, owner, dp))
    out_specs = P(None, owner, dp)
    return jax.shard_map(body, mesh=fine, in_specs=in_specs, out_specs=out_specs, check_vma=False)
```

```python
import jax
import jax.numpy as jnp
from jax import lax
from jax.experimental import pallas as pl
from jax.experimental.pallas import tpu as pltpu
from jax.sharding import Mesh, PartitionSpec as P

BLK = 512
SUB = 128
damping = 0.1
TOKENS = 4096
F32 = jnp.float32
BF16 = jnp.bfloat16
VMEM = pltpu.VMEM

PAIRS = [(r, c) for r in range(4) for c in range(r, 4)]
LANES = 15 * SUB


def tn_dot(a, b):
    return lax.dot_general(a, b, (((0,), (0,)), ((), ())), preferred_element_type=F32)


def nn_dot(a, b):
    return lax.dot_general(a, b, (((1,), (0,)), ((), ())), preferred_element_type=F32)


def cov_kernel(pos, acts, grads, h0, h1, h2, h3, pack):
    y, part = pos[1], pos[3]
    sends = (h0, h1, h2, h3)
    for layer in range(2):
        for b in range(3):
            rows = grads[layer, :, b * BLK:(b + 1) * BLK]
            top = tn_dot(rows[:, :256], rows).astype(BF16)
            low = tn_dot(rows[:, 256:], rows[:, 256:]).astype(BF16)
            for i, (r, c) in enumerate(PAIRS):
                s = 10 * b + i
                if r < 2:
                    piece = top[r * SUB:(r + 1) * SUB, c * SUB:(c + 1) * SUB]
                else:
                    piece = low[(r - 2) * SUB:(r - 1) * SUB, (c - 2) * SUB:(c - 1) * SUB]
                pack[layer, s // 15 * SUB:(s // 15 + 1) * SUB, s % 15 * SUB:(s % 15 + 1) * SUB] = piece
    for d in range(4):
        at = pl.multiple_of((y + d) % 4 * 64, 64)
        sends[d][0:64, :] = pack[0, pl.ds(at, 64), :]
        sends[d][64:128, :] = pack[1, pl.ds(at, 64), :]
    k = lax.broadcasted_iota(jnp.int32, (BLK, 64), 0)
    m = lax.broadcasted_iota(jnp.int32, (BLK, 64), 1)
    select = jnp.where(k == m // 16 * SUB + part * 16 + m % 16, 1.0, 0.0).astype(BF16)
    for d in range(4):
        start = (y + d) % 4 * (3 * BLK)
        for j in range(3):
            rows = acts[0, :, pl.ds(pl.multiple_of(start + j * BLK, BLK), BLK)]
            chosen = nn_dot(rows, select).astype(BF16)
            cov = tn_dot(chosen, rows).astype(BF16)
            for i, (r, c) in enumerate(PAIRS):
                s = 10 * j + i
                sends[d][128 + s // 15 * 16:144 + s // 15 * 16, s % 15 * SUB:(s % 15 + 1) * SUB] = (
                    cov[r * 16:(r + 1) * 16, c * SUB:(c + 1) * SUB]
                )


def invert(packed_piece, full):
    for i, (r, c) in enumerate(PAIRS):
        piece = packed_piece(i).astype(F32)
        full[r * SUB:(r + 1) * SUB, c * SUB:(c + 1) * SUB] = piece
        if r != c:
            full[c * SUB:(c + 1) * SUB, r * SUB:(r + 1) * SUB] = piece.T
    ri = lax.broadcasted_iota(jnp.int32, (BLK, BLK), 0)
    ci = lax.broadcasted_iota(jnp.int32, (BLK, BLK), 1)
    diagonal = ri == ci
    matrix = full[...] + jnp.where(diagonal, damping, 0.0)
    two_eye = jnp.where(diagonal, 2.0, 0.0)
    sums = jnp.sum(jnp.abs(matrix), axis=0, keepdims=True)
    alpha = (1.0 / jnp.max(sums, axis=1, keepdims=True)).astype(BF16).astype(F32)
    low = matrix.astype(BF16)
    residue = (two_eye - low.astype(F32) * alpha).astype(BF16)
    iterate = (residue.astype(F32) * alpha).astype(BF16)
    image = nn_dot(low, iterate)
    residue = (two_eye - image).astype(BF16)
    return nn_dot(iterate, residue).astype(BF16)


def right_kernel(pos, mine, other, w_own, w_pair, w_mid, out, pack, full, diag):
    x, core = pos[0], pos[2]
    for q in range(4):
        at = pl.multiple_of(q * 32 + core * 16, 16)
        pack[pl.ds(at, 16), :] = mine[q * 16:(q + 1) * 16, :]
        at = pl.multiple_of(q * 32 + (1 - core) * 16, 16)
        pack[pl.ds(at, 16), :] = other[q * 16:(q + 1) * 16, :]
    base = x // 2 * BLK
    own = pl.multiple_of(x * 384 - base, SUB)
    pair = pl.multiple_of((x + 1 - 2 * (x % 2)) * 384 - base, SUB)
    mid = pl.multiple_of(jnp.where(x == 1, 768, 0), SUB)
    for b in range(2):
        at = b * BLK
        inverse = invert(lambda i: pack[:, b * 1280 + i * SUB:b * 1280 + (i + 1) * SUB], full.at[b])
        diag[at:at + BLK, at:at + BLK] = inverse
        diag[at:at + BLK, BLK - at:2 * BLK - at] = jnp.zeros((BLK, BLK), BF16)
    columns = pl.ds(own, 384)
    total = nn_dot(w_own[0], diag[pl.ds(own, 384), columns])
    total += nn_dot(w_pair[...], diag[pl.ds(pair, 384), columns])
    total += nn_dot(w_mid[0], diag[pl.ds(mid, 256), columns])
    out[...] = total.astype(BF16)


def right(pos, sides, other, weight_grad, w_pair, w_mid, layer):
    rows = pl.BlockSpec((64, 2560), lambda i, p: (layer, 0))
    shape = jax.ShapeDtypeStruct(weight_grad.shape[1:], BF16)
    return call(
        right_kernel, pos, (sides, other, weight_grad, w_pair, w_mid),
        [rows, rows, of_layer(weight_grad, layer), whole(w_pair), of_layer(w_mid, layer)], [shape],
        [VMEM((128, 2560), BF16), VMEM((2, BLK, BLK), F32), VMEM((1024, 1024), BF16)], 2_500_000_000,
    )[0]


def left_kernel(pos, p0, p1, p2, p3, right, *refs):
    out, pack, full = refs[-3:]
    x, y = pos[0], pos[1]
    for d, part in enumerate((p0, p1, p2, p3)):
        for e in range(4):
            at = (y + 4 - d) % 4 * 64 + (x + 4 - e) % 4 * 16
            pack[pl.ds(pl.multiple_of(at, 16), 16), :] = part[e * 16:(e + 1) * 16, :]
    for b in range(3):
        def piece(i):
            s = 10 * b + i
            return pack[s // 15 * SUB:(s // 15 + 1) * SUB, s % 15 * SUB:(s % 15 + 1) * SUB]
        inverse = invert(piece, full.at[b])
        at = b * BLK
        out[0, at:at + BLK, :] = nn_dot(inverse, right[at:at + BLK, :]).astype(BF16)


def left(pos, parts, right, layer, before):
    operands = [*parts, right]
    in_specs = [whole(a) for a in operands]
    if before is not None:
        operands.append(before)
        in_specs.append(pl.BlockSpec(memory_space=pl.ANY))
    shape = jax.ShapeDtypeStruct((2,) + right.shape, BF16)
    return call(
        left_kernel, pos, operands, in_specs, [shape],
        [VMEM((256, LANES), BF16), VMEM((3, BLK, BLK), F32)], 2_500_000_000,
        out_specs=[of_layer(shape, layer)], aliases={} if before is None else {len(operands): 0},
    )[0]


def call(kernel, pos, operands, in_specs, out_shape, scratch, flops, out_specs=None, aliases={}):
    return pl.pallas_call(
        kernel,
        grid_spec=pltpu.PrefetchScalarGridSpec(
            num_scalar_prefetch=1,
            grid=(1,),
            in_specs=in_specs,
            out_specs=out_specs or [whole(s) for s in out_shape],
            scratch_shapes=scratch,
        ),
        out_shape=out_shape,
        input_output_aliases=aliases,
        compiler_params=pltpu.CompilerParams(vmem_limit_bytes=48 * 1024 * 1024),
        cost_estimate=pl.CostEstimate(flops=flops, bytes_accessed=8_000_000, transcendentals=0),
    )(pos, *operands)


def whole(a):
    return pl.BlockSpec(a.shape, lambda i, p, n=len(a.shape): (0,) * n)


def of_layer(a, layer):
    return pl.BlockSpec((1,) + a.shape[1:], lambda i, p: (layer, 0, 0))


def shift(a, axis, d):
    return lax.ppermute(a, axis, [(i, (i + d) % 4) for i in range(4)])


def add(parts):
    return sum(p.astype(F32) for p in parts)


def spread(parts, axis):
    return [parts[0]] + [shift(parts[d], axis, d) for d in (1, 2, 3)]


def gather(a, axis):
    return [a] + [shift(a, axis, d) for d in (1, 2, 3)]


def chunk(a, index, rows):
    return lax.dynamic_slice_in_dim(a, index % 4 * rows, rows, 0)


def body(acts, grads_out, weight_grad):
    y, x, z, c = (lax.axis_index(n) for n in ("y", "x", "z", "c"))
    part = z % 4 * 2 + c
    pos = jnp.stack([x, y, c, part, z // 4]).astype(jnp.int32)

    w_pair = [lax.ppermute(weight_grad[n], "x", [(0, 1), (1, 0), (2, 3), (3, 2)]) for n in range(2)]
    middle = lax.dynamic_slice_in_dim(weight_grad, jnp.where(x == 1, SUB, 0), 256, 2)
    w_mid = lax.ppermute(middle, "x", [(1, 2), (2, 1)])

    covs = call(
        cov_kernel, pos, (acts, grads_out),
        [pl.BlockSpec((1, 256, 6144), lambda i, p: (p[4], 0, 0)), whole(grads_out)],
        [jax.ShapeDtypeStruct((160, LANES), BF16)] * 4, [VMEM((2, 256, LANES), BF16)], 3_000_000_000,
    )
    rows = add(spread(covs, "y")).astype(BF16)
    rows, w_mid, w_pair[0] = lax.optimization_barrier((rows, w_mid, w_pair[0]))
    sends = [
        jnp.concatenate([chunk(rows[:64], x + d, 16), chunk(rows[64:128], x + d, 16), rows[128:]], axis=0)
        for d in range(4)
    ]
    rows = add(spread(sends, "x")) * (1.0 / TOKENS)
    side = jnp.concatenate([rows[32:48], rows[48:64]], axis=1)
    side = lax.dynamic_slice_in_dim(side, x // 2 * 1280, 2560, 1).astype(BF16)

    quarter = gather(rows[:32].astype(BF16), "x")
    first = gather(jnp.concatenate([q[:16] for q in quarter], axis=0), "y")
    second = gather(jnp.concatenate([q[16:] for q in quarter], axis=0), "y")
    sides = lax.all_to_all(jnp.tile(side, (8, 1)), "z", 0, 0, tiled=True)
    other = lax.ppermute(sides, "c", [(0, 1), (1, 0)])

    out = left(pos, first, right(pos, sides, other, weight_grad, w_pair[0], w_mid, 0), 0, None)
    return left(pos, second, right(pos, sides, other, weight_grad, w_pair[1], w_mid, 1), 1, out)


def solution(mesh):
    fine = Mesh(mesh.devices.reshape(4, 4, 8, 2), ("y", "x", "z", "c"))
    dp, owner = ("y", "x"), ("z", "c")
    in_specs = (P(None, dp, None), P(None, dp, owner), P(None, owner, dp))
    out_specs = P(None, owner, dp)
    return jax.shard_map(body, mesh=fine, in_specs=in_specs, out_specs=out_specs, check_vma=False)
```

```python
import jax
import jax.numpy as jnp
from jax import lax
from jax.experimental import pallas as pl
from jax.experimental.pallas import tpu as pltpu
from jax.sharding import Mesh, PartitionSpec as P

BLK = 512
SUB = 128
damping = 0.1
TOKENS = 4096
F32 = jnp.float32
BF16 = jnp.bfloat16
VMEM = pltpu.VMEM

PAIRS = [(r, c) for r in range(4) for c in range(r, 4)]
LANES = 15 * SUB


def tn_dot(a, b):
    return lax.dot_general(a, b, (((0,), (0,)), ((), ())), preferred_element_type=F32)


def nn_dot(a, b):
    return lax.dot_general(a, b, (((1,), (0,)), ((), ())), preferred_element_type=F32)


def side_kernel(pos, acts, s0, s1, s2, s3):
    y, part = pos[1], pos[3]
    k = lax.broadcasted_iota(jnp.int32, (BLK, 64), 0)
    m = lax.broadcasted_iota(jnp.int32, (BLK, 64), 1)
    select = jnp.where(k == m // 16 * SUB + part * 16 + m % 16, 1.0, 0.0).astype(BF16)
    for d, send in enumerate((s0, s1, s2, s3)):
        start = (y + d) % 4 * (3 * BLK)
        for j in range(3):
            rows = acts[0, :, pl.ds(pl.multiple_of(start + j * BLK, BLK), BLK)]
            chosen = nn_dot(rows, select).astype(BF16)
            cov = tn_dot(chosen, rows).astype(BF16)
            for i, (r, c) in enumerate(PAIRS):
                s = 10 * j + i
                send[s // 15 * 16:(s // 15 + 1) * 16, s % 15 * SUB:(s % 15 + 1) * SUB] = (
                    cov[r * 16:(r + 1) * 16, c * SUB:(c + 1) * SUB]
                )


def cov_kernel(pos, t0, t1, t2, t3, c0, c1, c2, c3, pack):
    x = pos[0]
    for b in range(3):
        top, low = 0.0, 0.0
        for tokens in (t0, t1, t2, t3):
            rows = tokens[:, b * BLK:(b + 1) * BLK]
            top += tn_dot(rows[:, :256], rows)
            low += tn_dot(rows[:, 256:], rows[:, 256:])
        top, low = top.astype(BF16), low.astype(BF16)
        for i, (r, c) in enumerate(PAIRS):
            if r < 2:
                piece = top[r * SUB:(r + 1) * SUB, c * SUB:(c + 1) * SUB]
            else:
                piece = low[(r - 2) * SUB:(r - 1) * SUB, (c - 2) * SUB:(c - 1) * SUB]
            pack[b, :, i * SUB:(i + 1) * SUB] = piece
    for d, send in enumerate((c0, c1, c2, c3)):
        send[...] = pack[jnp.minimum((x + d) % 4, 2)]


def unpack(piece, full):
    for i, (r, c) in enumerate(PAIRS):
        tile = piece(i)
        full[r * SUB:(r + 1) * SUB, c * SUB:(c + 1) * SUB] = tile.astype(full.dtype)
        if r != c:
            full[c * SUB:(c + 1) * SUB, r * SUB:(r + 1) * SUB] = tile.T.astype(full.dtype)


def invert(full):
    ri = lax.broadcasted_iota(jnp.int32, (BLK, BLK), 0)
    ci = lax.broadcasted_iota(jnp.int32, (BLK, BLK), 1)
    diagonal = ri == ci
    matrix = full[...] + jnp.where(diagonal, damping, 0.0)
    two_eye = jnp.where(diagonal, 2.0, 0.0)
    sums = jnp.sum(jnp.abs(matrix), axis=0, keepdims=True)
    alpha = (1.0 / jnp.max(sums, axis=1, keepdims=True)).astype(BF16).astype(F32)
    low = matrix.astype(BF16)
    residue = (two_eye - low.astype(F32) * alpha).astype(BF16)
    iterate = (residue.astype(F32) * alpha).astype(BF16)
    image = nn_dot(low, iterate)
    residue = (two_eye - image).astype(BF16)
    return nn_dot(iterate, residue).astype(BF16)


def newton_kernel(pos, c0, c1, c2, c3, out, full):
    def piece(i):
        at = slice(i * SUB, (i + 1) * SUB)
        return sum(c[:, at].astype(F32) for c in (c0, c1, c2, c3)) * (1.0 / TOKENS)

    unpack(piece, full)
    inverse = invert(full)
    for i, (r, c) in enumerate(PAIRS):
        out[:, i * SUB:(i + 1) * SUB] = inverse[r * SUB:(r + 1) * SUB, c * SUB:(c + 1) * SUB]


def factor_kernel(pos, mine, other, out, pack, full, diag):
    x, core = pos[0], pos[2]
    base = x // 2 * BLK
    own = pl.multiple_of(x * 384 - base, SUB)
    pair = pl.multiple_of((x + 1 - 2 * (x % 2)) * 384 - base, SUB)
    mid = pl.multiple_of(jnp.where(x == 1, 768, 0), SUB)
    columns = pl.ds(own, 384)
    for layer in range(2):
        for q in range(4):
            z = 4 * layer + q
            at = pl.multiple_of(q * 32 + core * 16, 16)
            pack[layer, pl.ds(at, 16), :] = mine[z * 16:(z + 1) * 16, :]
            at = pl.multiple_of(q * 32 + (1 - core) * 16, 16)
            pack[layer, pl.ds(at, 16), :] = other[z * 16:(z + 1) * 16, :]
        for b in range(2):
            at = b * BLK
            unpack(
                lambda i: pack[layer, :, b * 1280 + i * SUB:b * 1280 + (i + 1) * SUB].astype(F32),
                full.at[layer, b],
            )
            diag[layer, at:at + BLK, at:at + BLK] = invert(full.at[layer, b])
            diag[layer, at:at + BLK, BLK - at:2 * BLK - at] = jnp.zeros((BLK, BLK), BF16)
        out[layer, 0:384, :] = diag[layer, pl.ds(own, 384), columns]
        out[layer, 384:768, :] = diag[layer, pl.ds(pair, 384), columns]
        out[layer, 768:1024, :] = diag[layer, pl.ds(mid, 256), columns]


def right_kernel(pos, w_own, w_pair, w_mid, factor, out):
    total = nn_dot(w_own[0], factor[0, 0:384, :])
    total += nn_dot(w_pair[...], factor[0, 384:768, :])
    total += nn_dot(w_mid[...], factor[0, 768:1024, :])
    out[...] = total.astype(BF16)


def left_kernel(pos, p0, p1, p2, p3, r0, r1, out, pack, full):
    y, core = pos[1], pos[2]
    for layer, right in enumerate((r0, r1)):
        shift_of = (y + 4 - 2 * core - layer) % 4
        for d, part in enumerate((p0, p1, p2, p3)):
            @pl.when(shift_of == d)
            def _():
                pack[...] = part[...]
        for b in range(3):
            unpack(
                lambda i: pack[b * SUB:(b + 1) * SUB, i * SUB:(i + 1) * SUB].astype(F32),
                full.at[layer, b],
            )
            at = b * BLK
            out[layer, at:at + BLK, :] = nn_dot(full[layer, b], right[at:at + BLK, :]).astype(BF16)


def call(kernel, pos, operands, in_specs, out_shape, scratch, flops, out_specs=None, aliases={}):
    return pl.pallas_call(
        kernel,
        grid_spec=pltpu.PrefetchScalarGridSpec(
            num_scalar_prefetch=1,
            grid=(1,),
            in_specs=in_specs,
            out_specs=out_specs or [whole(s) for s in out_shape],
            scratch_shapes=scratch,
        ),
        out_shape=out_shape,
        input_output_aliases=aliases,
        compiler_params=pltpu.CompilerParams(vmem_limit_bytes=48 * 1024 * 1024),
        cost_estimate=pl.CostEstimate(flops=flops, bytes_accessed=8_000_000, transcendentals=0),
    )(pos, *operands)


def whole(a):
    return pl.BlockSpec(a.shape, lambda i, p, n=len(a.shape): (0,) * n)


def of_layer(a, layer):
    return pl.BlockSpec((1,) + a.shape[1:], lambda i, p: (layer, 0, 0))


def add(parts):
    return sum(p.astype(F32) for p in parts)


def send(a, axes, links):
    return lax.ppermute(a, axes, links)


def ring(d):
    return [(i, (i + d) % 4) for i in range(4)]


def to_handler(d):
    return [(y * 2 + c, (y + d) % 4 * 2 + c) for y in range(4) for c in range(2) if (y + d) % 4 // 2 == c]


def from_handler(d):
    return [(y * 2 + c, (y + d) % 4 * 2 + c) for y in range(4) for c in range(2) if y // 2 == c]


def along_x(d, source, target):
    return [
        ((y * 4 + x) * 2 + y // 2, (y * 4 + (x + d) % 4) * 2 + y // 2)
        for y in range(4) for x in range(4) if x < source and (x + d) % 4 < target
    ]


def body(acts, grads_out, weight_grad):
    y, x, z, c = (lax.axis_index(n) for n in ("y", "x", "z", "c"))
    pos = jnp.stack([x, y, c, z % 4 * 2 + c, z // 4]).astype(jnp.int32)
    shifts = (1, 2, 3)

    odd = lax.dynamic_index_in_dim(grads_out, (y + 1) % 2, 0, False)
    even = lax.dynamic_index_in_dim(grads_out, y % 2, 0, False)
    tokens = [even] + [send(even if d == 2 else odd, ("y", "c"), to_handler(d)) for d in shifts]

    def exchange(w):
        middle = lax.dynamic_slice_in_dim(w, jnp.where(x == 1, SUB, 0), 256, 1)
        return [send(w, "x", [(0, 1), (1, 0), (2, 3), (3, 2)]), send(middle, "x", [(1, 2), (2, 1)])]

    w_first = exchange(weight_grad[0])

    sides = call(
        side_kernel, pos, (acts,), [pl.BlockSpec((1, 256, 6144), lambda i, p: (p[4], 0, 0))],
        [jax.ShapeDtypeStruct((32, LANES), BF16)] * 4, [], 1_000_000_000,
    )
    side = add([sides[0]] + [send(sides[d], "y", ring(d)) for d in shifts]).astype(BF16)

    covs = call(
        cov_kernel, pos, tokens, [whole(t) for t in tokens],
        [jax.ShapeDtypeStruct((SUB, 1280), BF16)] * 4, [VMEM((3, SUB, 1280), BF16)], 1_500_000_000,
    )
    side, covs, w_first = lax.optimization_barrier((side, covs, w_first))
    covs = [covs[0]] + [send(covs[d], ("y", "x", "c"), along_x(d, 4, 3)) for d in shifts]
    side = add([side] + [send(side, "x", ring(d)) for d in shifts]) * (1.0 / TOKENS)
    side = jnp.concatenate([side[:16], side[16:]], axis=1)
    side = lax.dynamic_slice_in_dim(side, x // 2 * 1280, 2560, 1).astype(BF16)

    inverse = call(
        newton_kernel, pos, covs, [whole(t) for t in covs],
        [jax.ShapeDtypeStruct((SUB, 1280), BF16)], [VMEM((BLK, BLK), F32)], 600_000_000,
    )[0]
    row = jnp.stack([inverse] + [send(inverse, ("y", "x", "c"), along_x(d, 3, 4)) for d in shifts])
    row = jnp.concatenate([lax.dynamic_index_in_dim(row, (x + 4 - b) % 4, 0, False) for b in range(3)], axis=0)

    row, w_second = lax.optimization_barrier((row, weight_grad[1]))
    parts = [row] + [send(row, ("y", "c"), from_handler(d)) for d in shifts]
    w_second = exchange(w_second)

    mine = lax.all_to_all(jnp.tile(side, (8, 1)), "z", 0, 0, tiled=True)
    other = lax.ppermute(mine, "c", [(0, 1), (1, 0)])
    factor = call(
        factor_kernel, pos, (mine, other), [whole(mine), whole(other)],
        [jax.ShapeDtypeStruct((2, 1024, 384), BF16)],
        [VMEM((2, SUB, 2560), BF16), VMEM((2, 2, BLK, BLK), F32), VMEM((2, 1024, 1024), BF16)], 2_500_000_000,
    )[0]
    rights = [
        call(
            right_kernel, pos, (weight_grad, *w, factor),
            [of_layer(weight_grad, layer), whole(w[0]), whole(w[1]), of_layer(factor, layer)],
            [jax.ShapeDtypeStruct(weight_grad.shape[1:], BF16)], [], 1_200_000_000,
        )[0]
        for layer, w in enumerate((w_first, w_second))
    ]
    operands = (*parts, *rights)
    return call(
        left_kernel, pos, operands, [whole(a) for a in operands],
        [jax.ShapeDtypeStruct(weight_grad.shape, BF16)],
        [VMEM((3 * SUB, 1280), BF16), VMEM((2, 3, BLK, BLK), BF16)], 1_500_000_000,
    )[0]


def solution(mesh):
    fine = Mesh(mesh.devices.reshape(4, 4, 8, 2), ("y", "x", "z", "c"))
    dp, owner = ("y", "x"), ("z", "c")
    in_specs = (P(None, dp, None), P(None, dp, owner), P(None, owner, dp))
    out_specs = P(None, owner, dp)
    return jax.shard_map(body, mesh=fine, in_specs=in_specs, out_specs=out_specs, check_vma=False)
```

```python
import jax
import jax.numpy as jnp
from jax import lax
from jax.experimental import pallas as pl
from jax.experimental.pallas import tpu as pltpu
from jax.sharding import Mesh, PartitionSpec as P

BLK = 512
SUB = 128
damping = 0.1
TOKENS = 4096
F32 = jnp.float32
BF16 = jnp.bfloat16
VMEM = pltpu.VMEM

PAIRS = [(r, c) for r in range(4) for c in range(r, 4)]
LANES = 15 * SUB


def tn_dot(a, b):
    return lax.dot_general(a, b, (((0,), (0,)), ((), ())), preferred_element_type=F32)


def nn_dot(a, b):
    return lax.dot_general(a, b, (((1,), (0,)), ((), ())), preferred_element_type=F32)


def token_kernel(pos, grads, odd, even, sems):
    y = pos[1]
    copies = [
        pltpu.make_async_copy(grads.at[(y + 1) % 2], odd, sems.at[0]),
        pltpu.make_async_copy(grads.at[y % 2], even, sems.at[1]),
    ]
    for copy in copies:
        copy.start()
    for copy in copies:
        copy.wait()


def columns_kernel(pos, w, whole0, mid0, whole1, mid1, sems):
    columns = pl.ds(pl.multiple_of(jnp.where(pos[0] == 1, SUB, 0), SUB), 256)
    copies = [
        pltpu.make_async_copy(w.at[0], whole0, sems.at[0]),
        pltpu.make_async_copy(w.at[0, :, columns], mid0, sems.at[1]),
        pltpu.make_async_copy(w.at[1], whole1, sems.at[2]),
        pltpu.make_async_copy(w.at[1, :, columns], mid1, sems.at[3]),
    ]
    for copy in copies:
        copy.start()
    for copy in copies:
        copy.wait()


def side_kernel(pos, acts, out):
    part = pos[3]
    k = lax.broadcasted_iota(jnp.int32, (BLK, 64), 0)
    m = lax.broadcasted_iota(jnp.int32, (BLK, 64), 1)
    select = jnp.where(k == m // 16 * SUB + part * 16 + m % 16, 1.0, 0.0).astype(BF16)
    for b in range(12):
        rows = acts[0, :, b * BLK:(b + 1) * BLK]
        chosen = nn_dot(rows, select).astype(BF16)
        cov = tn_dot(chosen, rows).astype(BF16)
        for i, (r, c) in enumerate(PAIRS):
            s = 10 * (b % 3) + i
            at = b // 3 * 32 + s // 15 * 16
            out[at:at + 16, s % 15 * SUB:(s % 15 + 1) * SUB] = cov[r * 16:(r + 1) * 16, c * SUB:(c + 1) * SUB]


def cov_kernel(pos, t0, t1, t2, t3, c0, c1, c2, c3, pack):
    x = pos[0]
    for b in range(3):
        top, low = 0.0, 0.0
        for tokens in (t0, t1, t2, t3):
            rows = tokens[:, b * BLK:(b + 1) * BLK]
            top += tn_dot(rows[:, :256], rows)
            low += tn_dot(rows[:, 256:], rows[:, 256:])
        top, low = top.astype(BF16), low.astype(BF16)
        for i, (r, c) in enumerate(PAIRS):
            if r < 2:
                piece = top[r * SUB:(r + 1) * SUB, c * SUB:(c + 1) * SUB]
            else:
                piece = low[(r - 2) * SUB:(r - 1) * SUB, (c - 2) * SUB:(c - 1) * SUB]
            pack[b, :, i * SUB:(i + 1) * SUB] = piece
    for d, send in enumerate((c0, c1, c2, c3)):
        send[...] = pack[jnp.minimum((x + d) % 4, 2)]


def unpack(piece, full):
    for i, (r, c) in enumerate(PAIRS):
        tile = piece(i)
        full[r * SUB:(r + 1) * SUB, c * SUB:(c + 1) * SUB] = tile.astype(full.dtype)
        if r != c:
            full[c * SUB:(c + 1) * SUB, r * SUB:(r + 1) * SUB] = tile.T.astype(full.dtype)


def invert(full):
    ri = lax.broadcasted_iota(jnp.int32, (BLK, BLK), 0)
    ci = lax.broadcasted_iota(jnp.int32, (BLK, BLK), 1)
    diagonal = ri == ci
    matrix = full[...] + jnp.where(diagonal, damping, 0.0)
    two_eye = jnp.where(diagonal, 2.0, 0.0)
    sums = jnp.sum(jnp.abs(matrix), axis=0, keepdims=True)
    alpha = (1.0 / jnp.max(sums, axis=1, keepdims=True)).astype(BF16).astype(F32)
    low = matrix.astype(BF16)
    residue = (two_eye - low.astype(F32) * alpha).astype(BF16)
    iterate = (residue.astype(F32) * alpha).astype(BF16)
    image = nn_dot(low, iterate)
    residue = (two_eye - image).astype(BF16)
    return nn_dot(iterate, residue).astype(BF16)


def newton_kernel(pos, c0, c1, c2, c3, out, full):
    def piece(i):
        at = slice(i * SUB, (i + 1) * SUB)
        return sum(c[:, at].astype(F32) for c in (c0, c1, c2, c3)) * (1.0 / TOKENS)

    unpack(piece, full)
    inverse = invert(full)
    for i, (r, c) in enumerate(PAIRS):
        out[:, i * SUB:(i + 1) * SUB] = inverse[r * SUB:(r + 1) * SUB, c * SUB:(c + 1) * SUB]


def row_kernel(pos, p0, p1, p2, p3, out):
    x = pos[0]
    for b in range(3):
        for d, part in enumerate((p0, p1, p2, p3)):
            @pl.when((x + 4 - b) % 4 == d)
            def _():
                out[b * SUB:(b + 1) * SUB, :] = part[...]


def factor_kernel(pos, mine, other, out, pack, full, diag):
    x, core = pos[0], pos[2]
    base = x // 2 * BLK
    own = pl.multiple_of(x * 384 - base, SUB)
    pair = pl.multiple_of((x + 1 - 2 * (x % 2)) * 384 - base, SUB)
    mid = pl.multiple_of(jnp.where(x == 1, 768, 0), SUB)
    columns = pl.ds(own, 384)
    for layer in range(2):
        for q in range(4):
            z = 4 * layer + q
            at = pl.multiple_of(q * 32 + core * 16, 16)
            pack[layer, pl.ds(at, 16), :] = mine[z * 16:(z + 1) * 16, :]
            at = pl.multiple_of(q * 32 + (1 - core) * 16, 16)
            pack[layer, pl.ds(at, 16), :] = other[z * 16:(z + 1) * 16, :]
        for b in range(2):
            at = b * BLK
            unpack(
                lambda i: pack[layer, :, b * 1280 + i * SUB:b * 1280 + (i + 1) * SUB].astype(F32),
                full.at[layer, b],
            )
            diag[layer, at:at + BLK, at:at + BLK] = invert(full.at[layer, b])
            diag[layer, at:at + BLK, BLK - at:2 * BLK - at] = jnp.zeros((BLK, BLK), BF16)
        out[layer, 0:384, :] = diag[layer, pl.ds(own, 384), columns]
        out[layer, 384:768, :] = diag[layer, pl.ds(pair, 384), columns]
        out[layer, 768:1024, :] = diag[layer, pl.ds(mid, 256), columns]


def right_product(w_own, w_pair, w_mid, factor):
    total = nn_dot(w_own[0], factor[0, 0:384, :])
    total += nn_dot(w_pair[...], factor[0, 384:768, :])
    total += nn_dot(w_mid[...], factor[0, 768:1024, :])
    return total.astype(BF16)


def right_kernel(pos, w_own, w_pair, w_mid, factor, out):
    out[...] = right_product(w_own, w_pair, w_mid, factor)


def left_product(pos, layer, parts, right, out, pack, full):
    y, core = pos[1], pos[2]
    for d, part in enumerate(parts):
        @pl.when((y + 4 - 2 * core - layer) % 4 == d)
        def _():
            pack[...] = part[...]
    for b in range(3):
        unpack(lambda i: pack[b * SUB:(b + 1) * SUB, i * SUB:(i + 1) * SUB].astype(F32), full.at[b])
        at = b * BLK
        out[0, at:at + BLK, :] = nn_dot(full[b], right[at:at + BLK, :]).astype(BF16)


def left_kernel(pos, p0, p1, p2, p3, right, out, pack, full):
    left_product(pos, 0, (p0, p1, p2, p3), right, out, pack, full)


def last_kernel(pos, p0, p1, p2, p3, w_own, w_pair, w_mid, factor, before, out, pack, full, right):
    right[...] = right_product(w_own, w_pair, w_mid, factor)
    left_product(pos, 1, (p0, p1, p2, p3), right, out, pack, full)


def call(kernel, pos, operands, in_specs, out_shape, scratch, flops, out_specs=None, aliases={}):
    return pl.pallas_call(
        kernel,
        grid_spec=pltpu.PrefetchScalarGridSpec(
            num_scalar_prefetch=1,
            grid=(1,),
            in_specs=in_specs,
            out_specs=out_specs or [whole(s) for s in out_shape],
            scratch_shapes=scratch,
        ),
        out_shape=out_shape,
        input_output_aliases=aliases,
        compiler_params=pltpu.CompilerParams(vmem_limit_bytes=24 * 1024 * 1024),
        cost_estimate=pl.CostEstimate(flops=flops, bytes_accessed=4_000_000, transcendentals=0),
    )(pos, *operands)


ANYWHERE = pl.BlockSpec(memory_space=pl.ANY)
ONCE = pl.Buffered(1)


def whole(a):
    return pl.BlockSpec(a.shape, lambda i, p, n=len(a.shape): (0,) * n, pipeline_mode=ONCE)


def of_layer(a, layer):
    return pl.BlockSpec((1,) + a.shape[1:], lambda i, p: (layer, 0, 0), pipeline_mode=ONCE)


def shape(*dims):
    return jax.ShapeDtypeStruct(dims, BF16)


def add(parts):
    return sum(p.astype(F32) for p in parts)


def send(a, axes, links):
    return lax.ppermute(a, axes, links)


def to_handler(d):
    return [(y * 2 + c, (y + d) % 4 * 2 + c) for y in range(4) for c in range(2) if (y + d) % 4 // 2 == c]


def from_handler(d):
    return [(y * 2 + c, (y + d) % 4 * 2 + c) for y in range(4) for c in range(2) if y // 2 == c]


def along_x(d, source, target):
    return [
        ((y * 4 + x) * 2 + y // 2, (y * 4 + (x + d) % 4) * 2 + y // 2)
        for y in range(4) for x in range(4) if x < source and (x + d) % 4 < target
    ]


def body(acts, grads_out, weight_grad):
    y, x, z, c = (lax.axis_index(n) for n in ("y", "x", "z", "c"))
    pos = jnp.stack([x, y, c, z % 4 * 2 + c, z // 4]).astype(jnp.int32)
    shifts = (1, 2, 3)
    tokens, hidden = grads_out.shape[1:]
    rows, width = weight_grad.shape[1:]
    barrier = lax.optimization_barrier

    odd, even = call(
        token_kernel, pos, (grads_out,), [ANYWHERE], [shape(tokens, hidden)] * 2,
        [pltpu.SemaphoreType.DMA((2,))], 0, out_specs=[ANYWHERE] * 2,
    )
    tokens = [even] + [send(even if d == 2 else odd, ("y", "c"), to_handler(d)) for d in shifts]

    w_ready, _ = barrier((weight_grad, odd))
    whole0, mid0, whole1, mid1 = call(
        columns_kernel, pos, (w_ready,), [ANYWHERE], [shape(rows, width), shape(rows, 256)] * 2,
        [pltpu.SemaphoreType.DMA((4,))], 0, out_specs=[ANYWHERE] * 4,
    )

    def exchange(w, middle):
        return [send(w, "x", [(0, 1), (1, 0), (2, 3), (3, 2)]), send(middle, "x", [(1, 2), (2, 1)])]

    w_first = exchange(whole0, mid0)

    acts, tokens[1] = barrier((acts, tokens[1]))
    side = call(
        side_kernel, pos, (acts,),
        [pl.BlockSpec((1,) + acts.shape[1:], lambda i, p: (p[4], 0, 0), pipeline_mode=ONCE)],
        [shape(128, LANES)], [], 1_000_000_000,
    )[0]
    side = lax.all_to_all(side, "y", 0, 0, tiled=True)
    side = add([side[32 * d:32 * (d + 1)] for d in range(4)]).astype(BF16)
    side, tokens[2], tokens[3] = barrier((side, tokens[2], tokens[3]))

    covs = call(
        cov_kernel, pos, tokens, [whole(t) for t in tokens],
        [shape(SUB, 1280)] * 4, [VMEM((3, SUB, 1280), BF16)], 1_500_000_000,
    )
    covs = [covs[0]] + [send(covs[d], ("y", "x", "c"), along_x(d, 4, 3)) for d in shifts]
    side, covs[1] = barrier((side, covs[1]))
    side = lax.all_to_all(jnp.tile(side, (4, 1)), "x", 0, 0, tiled=True)
    side = add([side[32 * d:32 * (d + 1)] for d in range(4)]) * (1.0 / TOKENS)
    side = jnp.concatenate([side[:16], side[16:]], axis=1)
    side = lax.dynamic_slice_in_dim(side, x // 2 * 1280, 2560, 1).astype(BF16)
    covs, w_first = barrier((covs, w_first))

    inverse = call(
        newton_kernel, pos, covs, [whole(t) for t in covs],
        [shape(SUB, 1280)], [VMEM((BLK, BLK), F32)], 600_000_000,
    )[0]
    parts = [inverse] + [send(inverse, ("y", "x", "c"), along_x(d, 3, 4)) for d in shifts]
    side, parts[1] = barrier((side, parts[1]))
    row = call(row_kernel, pos, parts, [whole(t) for t in parts], [shape(3 * SUB, 1280)], [], 0)[0]

    row, whole1, mid1 = barrier((row, whole1, mid1))
    parts = [row] + [send(row, ("y", "c"), from_handler(d)) for d in shifts]
    w_second = exchange(whole1, mid1)

    mine = lax.all_to_all(jnp.tile(side, (8, 1)), "z", 0, 0, tiled=True)
    other = lax.ppermute(mine, "c", [(0, 1), (1, 0)])
    factor = call(
        factor_kernel, pos, (mine, other), [whole(mine), whole(other)], [shape(2, 1024, 384)],
        [VMEM((2, SUB, 2560), BF16), VMEM((2, 2, BLK, BLK), F32), VMEM((2, 1024, 1024), BF16)], 2_500_000_000,
    )[0]

    def products(layer, w):
        specs = [of_layer(weight_grad, layer), whole(w[0]), whole(w[1]), of_layer(factor, layer)]
        return (weight_grad, *w, factor), specs

    out = shape(*weight_grad.shape)
    scratch = [VMEM((3 * SUB, 1280), BF16), VMEM((3, BLK, BLK), BF16)]
    operands, specs = products(0, w_first)
    right = call(right_kernel, pos, operands, specs, [shape(rows, width)], [], 1_200_000_000)[0]
    operands = (*parts, right)
    before = call(
        left_kernel, pos, operands, [whole(a) for a in operands], [out], scratch, 600_000_000,
        out_specs=[of_layer(out, 0)],
    )[0]
    operands, specs = products(1, w_second)
    return call(
        last_kernel, pos, (*parts, *operands, before), [whole(a) for a in parts] + specs + [ANYWHERE], [out],
        scratch + [VMEM((rows, width), BF16)], 1_800_000_000, out_specs=[of_layer(out, 1)], aliases={9: 0},
    )[0]


def solution(mesh):
    fine = Mesh(mesh.devices.reshape(4, 4, 8, 2), ("y", "x", "z", "c"))
    dp, owner = ("y", "x"), ("z", "c")
    in_specs = (P(None, dp, None), P(None, dp, owner), P(None, owner, dp))
    out_specs = P(None, owner, dp)
    return jax.shard_map(body, mesh=fine, in_specs=in_specs, out_specs=out_specs, check_vma=False)
```

```python
import jax
import jax.numpy as jnp
from jax import lax
from jax.experimental import pallas as pl
from jax.experimental.pallas import tpu as pltpu
from jax.sharding import Mesh, PartitionSpec as P

BLK = 512
SUB = 128
damping = 0.1
TOKENS = 4096
F32 = jnp.float32
BF16 = jnp.bfloat16
VMEM = pltpu.VMEM

PAIRS = [(r, c) for r in range(4) for c in range(r, 4)]
LANES = 15 * SUB


def tn_dot(a, b):
    return lax.dot_general(a, b, (((0,), (0,)), ((), ())), preferred_element_type=F32)


def nn_dot(a, b):
    return lax.dot_general(a, b, (((1,), (0,)), ((), ())), preferred_element_type=F32)


def columns_kernel(pos, w, whole0, mid0, whole1, mid1, sems):
    columns = pl.ds(pl.multiple_of(jnp.where(pos[0] == 1, SUB, 0), SUB), 256)
    copies = [
        pltpu.make_async_copy(w.at[0], whole0, sems.at[0]),
        pltpu.make_async_copy(w.at[0, :, columns], mid0, sems.at[1]),
        pltpu.make_async_copy(w.at[1], whole1, sems.at[2]),
        pltpu.make_async_copy(w.at[1, :, columns], mid1, sems.at[3]),
    ]
    for copy in copies:
        copy.start()
    for copy in copies:
        copy.wait()


def side_kernel(pos, acts, out):
    part = pos[3]
    k = lax.broadcasted_iota(jnp.int32, (BLK, 64), 0)
    m = lax.broadcasted_iota(jnp.int32, (BLK, 64), 1)
    select = jnp.where(k == m // 16 * SUB + part * 16 + m % 16, 1.0, 0.0).astype(BF16)
    for b in range(12):
        rows = acts[0, :, b * BLK:(b + 1) * BLK]
        chosen = nn_dot(rows, select).astype(BF16)
        cov = tn_dot(chosen, rows).astype(BF16)
        for i, (r, c) in enumerate(PAIRS):
            s = 10 * (b % 3) + i
            at = b // 3 * 32 + s // 15 * 16
            out[at:at + 16, s % 15 * SUB:(s % 15 + 1) * SUB] = cov[r * 16:(r + 1) * 16, c * SUB:(c + 1) * SUB]


def cov_kernel(pos, grads, h0, h1, h2, h3, pack):
    y = pos[1]
    for layer in range(2):
        for b in range(3):
            rows = grads[layer, :, b * BLK:(b + 1) * BLK]
            top = tn_dot(rows[:, :256], rows).astype(BF16)
            low = tn_dot(rows[:, 256:], rows[:, 256:]).astype(BF16)
            for i, (r, c) in enumerate(PAIRS):
                s = 10 * b + i
                if r < 2:
                    piece = top[r * SUB:(r + 1) * SUB, c * SUB:(c + 1) * SUB]
                else:
                    piece = low[(r - 2) * SUB:(r - 1) * SUB, (c - 2) * SUB:(c - 1) * SUB]
                pack[layer, s // 15 * SUB:(s // 15 + 1) * SUB, s % 15 * SUB:(s % 15 + 1) * SUB] = piece
    for d, out in enumerate((h0, h1, h2, h3)):
        at = pl.multiple_of((y + d) % 4 * 64, 64)
        out[0:64, :] = pack[0, pl.ds(at, 64), :]
        out[64:128, :] = pack[1, pl.ds(at, 64), :]


def unpack(piece, full):
    for i, (r, c) in enumerate(PAIRS):
        tile = piece(i)
        full[r * SUB:(r + 1) * SUB, c * SUB:(c + 1) * SUB] = tile.astype(full.dtype)
        if r != c:
            full[c * SUB:(c + 1) * SUB, r * SUB:(r + 1) * SUB] = tile.T.astype(full.dtype)


def invert(full):
    ri = lax.broadcasted_iota(jnp.int32, (BLK, BLK), 0)
    ci = lax.broadcasted_iota(jnp.int32, (BLK, BLK), 1)
    diagonal = ri == ci
    matrix = full[...] + jnp.where(diagonal, damping, 0.0)
    two_eye = jnp.where(diagonal, 2.0, 0.0)
    sums = jnp.sum(jnp.abs(matrix), axis=0, keepdims=True)
    alpha = (1.0 / jnp.max(sums, axis=1, keepdims=True)).astype(BF16).astype(F32)
    low = matrix.astype(BF16)
    residue = (two_eye - low.astype(F32) * alpha).astype(BF16)
    iterate = (residue.astype(F32) * alpha).astype(BF16)
    image = nn_dot(low, iterate)
    residue = (two_eye - image).astype(BF16)
    return nn_dot(iterate, residue).astype(BF16)


def factor_kernel(pos, mine, other, out, pack, full, diag):
    x, core = pos[0], pos[2]
    base = x // 2 * BLK
    own = pl.multiple_of(x * 384 - base, SUB)
    pair = pl.multiple_of((x + 1 - 2 * (x % 2)) * 384 - base, SUB)
    mid = pl.multiple_of(jnp.where(x == 1, 768, 0), SUB)
    columns = pl.ds(own, 384)
    for layer in range(2):
        for q in range(4):
            z = 4 * layer + q
            at = pl.multiple_of(q * 32 + core * 16, 16)
            pack[layer, pl.ds(at, 16), :] = mine[z * 16:(z + 1) * 16, :]
            at = pl.multiple_of(q * 32 + (1 - core) * 16, 16)
            pack[layer, pl.ds(at, 16), :] = other[z * 16:(z + 1) * 16, :]
        for b in range(2):
            at = b * BLK
            unpack(
                lambda i: pack[layer, :, b * 1280 + i * SUB:b * 1280 + (i + 1) * SUB].astype(F32),
                full.at[layer, b],
            )
            diag[layer, at:at + BLK, at:at + BLK] = invert(full.at[layer, b])
            diag[layer, at:at + BLK, BLK - at:2 * BLK - at] = jnp.zeros((BLK, BLK), BF16)
        out[layer, 0:384, :] = diag[layer, pl.ds(own, 384), columns]
        out[layer, 384:768, :] = diag[layer, pl.ds(pair, 384), columns]
        out[layer, 768:1024, :] = diag[layer, pl.ds(mid, 256), columns]


def right_product(w_own, w_pair, w_mid, factor):
    total = nn_dot(w_own[0], factor[0, 0:384, :])
    total += nn_dot(w_pair[...], factor[0, 384:768, :])
    total += nn_dot(w_mid[...], factor[0, 768:1024, :])
    return total.astype(BF16)


def right_kernel(pos, w_own, w_pair, w_mid, factor, out):
    out[...] = right_product(w_own, w_pair, w_mid, factor)


def left_product(pos, layer, parts, right, out, pack, full):
    x, y = pos[0], pos[1]
    for d, part in enumerate(parts):
        for e in range(4):
            at = (y + 4 - d) % 4 * 64 + (x + 4 - e) % 4 * 16
            rows = 32 * e + 16 * layer
            pack[pl.ds(pl.multiple_of(at, 16), 16), :] = part[rows:rows + 16, :]
    for b in range(3):
        def piece(i):
            s = 10 * b + i
            return pack[s // 15 * SUB:(s // 15 + 1) * SUB, s % 15 * SUB:(s % 15 + 1) * SUB].astype(F32)

        unpack(piece, full.at[b])
        at = b * BLK
        out[0, at:at + BLK, :] = nn_dot(invert(full.at[b]), right[at:at + BLK, :]).astype(BF16)


def left_kernel(pos, p0, p1, p2, p3, right, out, pack, full):
    left_product(pos, 0, (p0, p1, p2, p3), right, out, pack, full)


def last_kernel(pos, p0, p1, p2, p3, w_own, w_pair, w_mid, factor, before, out, pack, full, right):
    right[...] = right_product(w_own, w_pair, w_mid, factor)
    left_product(pos, 1, (p0, p1, p2, p3), right, out, pack, full)


def call(kernel, pos, operands, in_specs, out_shape, scratch, out_specs=None, aliases={}):
    return pl.pallas_call(
        kernel,
        grid_spec=pltpu.PrefetchScalarGridSpec(
            num_scalar_prefetch=1,
            grid=(1,),
            in_specs=in_specs,
            out_specs=out_specs or [whole(s) for s in out_shape],
            scratch_shapes=scratch,
        ),
        out_shape=out_shape,
        input_output_aliases=aliases,
        compiler_params=pltpu.CompilerParams(vmem_limit_bytes=24 * 1024 * 1024),
        cost_estimate=pl.CostEstimate(flops=0, bytes_accessed=0, transcendentals=0),
    )(pos, *operands)


ANYWHERE = pl.BlockSpec(memory_space=pl.ANY)
ONCE = pl.Buffered(1)


def whole(a):
    return pl.BlockSpec(a.shape, lambda i, p, n=len(a.shape): (0,) * n, pipeline_mode=ONCE)


def of_layer(a, layer):
    return pl.BlockSpec((1,) + a.shape[1:], lambda i, p: (layer, 0, 0), pipeline_mode=ONCE)


def shape(*dims):
    return jax.ShapeDtypeStruct(dims, BF16)


def add(parts):
    return sum(p.astype(F32) for p in parts)


def spread(parts, axis):
    return [parts[0]] + [lax.ppermute(parts[d], axis, [(i, (i + d) % 4) for i in range(4)]) for d in (1, 2, 3)]


def chunk(a, index, rows):
    return lax.dynamic_slice_in_dim(a, index % 4 * rows, rows, 0)


def exchange(w, middle):
    pair = lax.ppermute(w, "x", [(0, 1), (1, 0), (2, 3), (3, 2)])
    return [pair, lax.ppermute(middle, "x", [(1, 2), (2, 1)])]


def body(acts, grads_out, weight_grad):
    y, x, z, c = (lax.axis_index(n) for n in ("y", "x", "z", "c"))
    pos = jnp.stack([x, y, c, z % 4 * 2 + c, z // 4]).astype(jnp.int32)
    rows, width = weight_grad.shape[1:]
    barrier = lax.optimization_barrier

    whole0, mid0, whole1, mid1 = call(
        columns_kernel, pos, (weight_grad,), [ANYWHERE], [shape(rows, width), shape(rows, 256)] * 2,
        [pltpu.SemaphoreType.DMA((4,))], out_specs=[ANYWHERE] * 4,
    )
    w_first = exchange(whole0, mid0)

    side = call(
        side_kernel, pos, (acts,),
        [pl.BlockSpec((1,) + acts.shape[1:], lambda i, p: (p[4], 0, 0), pipeline_mode=ONCE)],
        [shape(128, LANES)], [],
    )[0]
    side, grads_out = barrier((side, grads_out))
    side = lax.all_to_all(side, "y", 0, 0, tiled=True)
    side = add([side[32 * d:32 * (d + 1)] for d in range(4)]).astype(BF16)
    side = lax.all_to_all(jnp.tile(side, (4, 1)), "x", 0, 0, tiled=True)
    side = add([side[32 * d:32 * (d + 1)] for d in range(4)]) * (1.0 / TOKENS)
    side = jnp.concatenate([side[:16], side[16:]], axis=1)
    side = lax.dynamic_slice_in_dim(side, x // 2 * 1280, 2560, 1).astype(BF16)
    mine = lax.all_to_all(jnp.tile(side, (8, 1)), "z", 0, 0, tiled=True)

    covs = call(
        cov_kernel, pos, (grads_out,), [whole(grads_out)],
        [shape(128, LANES)] * 4, [VMEM((2, 256, LANES), BF16)],
    )
    quarter = add(spread(covs, "y")).astype(BF16)
    quarter, mine, w_first = barrier((quarter, mine, w_first))
    quarter = [
        jnp.concatenate([chunk(quarter[:64], x + d, 16), chunk(quarter[64:], x + d, 16)], axis=0) for d in range(4)
    ]
    own = (add(spread(quarter, "x")) * (1.0 / TOKENS)).astype(BF16)
    quarter = jnp.concatenate(spread([own] * 4, "x"), axis=0)
    quarter, whole1, mid1 = barrier((quarter, whole1, mid1))
    w_second = exchange(whole1, mid1)
    parts = spread([quarter] * 4, "y")

    other = lax.ppermute(mine, "c", [(0, 1), (1, 0)])
    factor = call(
        factor_kernel, pos, (mine, other), [whole(mine), whole(other)], [shape(2, 1024, 384)],
        [VMEM((2, SUB, 2560), BF16), VMEM((2, 2, BLK, BLK), F32), VMEM((2, 1024, 1024), BF16)],
    )[0]

    def products(layer, w):
        specs = [of_layer(weight_grad, layer), whole(w[0]), whole(w[1]), of_layer(factor, layer)]
        return (weight_grad, *w, factor), specs

    out = shape(*weight_grad.shape)
    scratch = [VMEM((256, LANES), BF16), VMEM((3, BLK, BLK), F32)]
    operands, specs = products(0, w_first)
    right = call(right_kernel, pos, operands, specs, [shape(rows, width)], [])[0]
    operands = (*parts, right)
    before = call(
        left_kernel, pos, operands, [whole(a) for a in operands], [out], scratch, out_specs=[of_layer(out, 0)]
    )[0]
    operands, specs = products(1, w_second)
    return call(
        last_kernel, pos, (*parts, *operands, before), [whole(a) for a in parts] + specs + [ANYWHERE], [out],
        scratch + [VMEM((rows, width), BF16)], out_specs=[of_layer(out, 1)], aliases={9: 0},
    )[0]


def solution(mesh):
    fine = Mesh(mesh.devices.reshape(4, 4, 8, 2), ("y", "x", "z", "c"))
    dp, owner = ("y", "x"), ("z", "c")
    in_specs = (P(None, dp, None), P(None, dp, owner), P(None, owner, dp))
    out_specs = P(None, owner, dp)
    return jax.shard_map(body, mesh=fine, in_specs=in_specs, out_specs=out_specs, check_vma=False)
```

```python
import jax
import jax.numpy as jnp
from jax import lax
from jax.experimental import pallas as pl
from jax.experimental.pallas import tpu as pltpu
from jax.sharding import Mesh, PartitionSpec as P

BLK = 512
SUB = 128
damping = 0.1
TOKENS = 4096
F32 = jnp.float32
BF16 = jnp.bfloat16
VMEM = pltpu.VMEM

PAIRS = [(r, c) for r in range(4) for c in range(r, 4)]
LANES = 15 * SUB


def tn_dot(a, b):
    return lax.dot_general(a, b, (((0,), (0,)), ((), ())), preferred_element_type=F32)


def nn_dot(a, b):
    return lax.dot_general(a, b, (((1,), (0,)), ((), ())), preferred_element_type=F32)


def columns_kernel(pos, w, whole0, whole1, mid, sems):
    columns = pl.ds(pl.multiple_of(jnp.where(pos[0] == 1, SUB, 0), SUB), 256)
    copies = [
        pltpu.make_async_copy(w.at[0], whole0, sems.at[0]),
        pltpu.make_async_copy(w.at[1], whole1, sems.at[1]),
        pltpu.make_async_copy(w.at[:, :, columns], mid, sems.at[2]),
    ]
    for copy in copies:
        copy.start()
    for copy in copies:
        copy.wait()


def side_kernel(pos, acts, out):
    part = pos[3]
    k = lax.broadcasted_iota(jnp.int32, (BLK, 64), 0)
    m = lax.broadcasted_iota(jnp.int32, (BLK, 64), 1)
    select = jnp.where(k == m // 16 * SUB + part * 16 + m % 16, 1.0, 0.0).astype(BF16)
    for b in range(12):
        rows = acts[0, :, b * BLK:(b + 1) * BLK]
        chosen = nn_dot(rows, select).astype(BF16)
        cov = tn_dot(chosen, rows).astype(BF16)
        for i, (r, c) in enumerate(PAIRS):
            s = 10 * (b % 3) + i
            at = b // 3 * 32 + s // 15 * 16
            out[at:at + 16, s % 15 * SUB:(s % 15 + 1) * SUB] = cov[r * 16:(r + 1) * 16, c * SUB:(c + 1) * SUB]


def cov_kernel(pos, grads, h0, h1, h2, h3, pack):
    y = pos[1]
    for layer in range(2):
        for b in range(3):
            rows = grads[layer, :, b * BLK:(b + 1) * BLK]
            top = tn_dot(rows[:, :256], rows).astype(BF16)
            low = tn_dot(rows[:, 256:], rows[:, 256:]).astype(BF16)
            for i, (r, c) in enumerate(PAIRS):
                s = 10 * b + i
                if r < 2:
                    piece = top[r * SUB:(r + 1) * SUB, c * SUB:(c + 1) * SUB]
                else:
                    piece = low[(r - 2) * SUB:(r - 1) * SUB, (c - 2) * SUB:(c - 1) * SUB]
                pack[layer, s // 15 * SUB:(s // 15 + 1) * SUB, s % 15 * SUB:(s % 15 + 1) * SUB] = piece
    for d, out in enumerate((h0, h1, h2, h3)):
        at = pl.multiple_of((y + d) % 4 * 64, 64)
        out[0:64, :] = pack[0, pl.ds(at, 64), :]
        out[64:128, :] = pack[1, pl.ds(at, 64), :]


def unpack(piece, full):
    for i, (r, c) in enumerate(PAIRS):
        tile = piece(i)
        full[r * SUB:(r + 1) * SUB, c * SUB:(c + 1) * SUB] = tile.astype(full.dtype)
        if r != c:
            full[c * SUB:(c + 1) * SUB, r * SUB:(r + 1) * SUB] = tile.T.astype(full.dtype)


def invert(full):
    ri = lax.broadcasted_iota(jnp.int32, (BLK, BLK), 0)
    ci = lax.broadcasted_iota(jnp.int32, (BLK, BLK), 1)
    diagonal = ri == ci
    matrix = full[...] + jnp.where(diagonal, damping, 0.0)
    two_eye = jnp.where(diagonal, 2.0, 0.0)
    sums = jnp.sum(jnp.abs(matrix), axis=0, keepdims=True)
    alpha = (1.0 / jnp.max(sums, axis=1, keepdims=True)).astype(BF16).astype(F32)
    low = matrix.astype(BF16)
    residue = (two_eye - low.astype(F32) * alpha).astype(BF16)
    iterate = (residue.astype(F32) * alpha).astype(BF16)
    image = nn_dot(low, iterate)
    residue = (two_eye - image).astype(BF16)
    return nn_dot(iterate, residue).astype(BF16)


def factor_kernel(pos, mine, other, out, pack, full, diag):
    x, core, zl = pos[0], pos[2], pos[5]
    base = x // 2 * BLK
    own = pl.multiple_of(x * 384 - base, SUB)
    pair = pl.multiple_of((x + 1 - 2 * (x % 2)) * 384 - base, SUB)
    mid = pl.multiple_of(jnp.where(x == 1, 768, 0), SUB)
    columns = pl.ds(own, 384)
    for layer in range(2):
        for q in range(4):
            parity = zl if q % 2 == 0 else 1 - zl
            rows = slice(64 * layer + 16 * q, 64 * layer + 16 * q + 16)
            at = pl.multiple_of(q // 2 * 64 + parity * 32 + core * 16, 16)
            pack[layer, pl.ds(at, 16), :] = mine[rows, :]
            at = pl.multiple_of(q // 2 * 64 + parity * 32 + (1 - core) * 16, 16)
            pack[layer, pl.ds(at, 16), :] = other[rows, :]
        for b in range(2):
            at = b * BLK
            unpack(
                lambda i: pack[layer, :, b * 1280 + i * SUB:b * 1280 + (i + 1) * SUB].astype(F32),
                full.at[layer, b],
            )
            diag[layer, at:at + BLK, at:at + BLK] = invert(full.at[layer, b])
            diag[layer, at:at + BLK, BLK - at:2 * BLK - at] = jnp.zeros((BLK, BLK), BF16)
        out[layer, 0:384, :] = diag[layer, pl.ds(own, 384), columns]
        out[layer, 384:768, :] = diag[layer, pl.ds(pair, 384), columns]
        out[layer, 768:1024, :] = diag[layer, pl.ds(mid, 256), columns]


def right_product(w_own, w_pair, w_mid, factor):
    total = nn_dot(w_own[0], factor[0, 0:384, :])
    total += nn_dot(w_pair[...], factor[0, 384:768, :])
    total += nn_dot(w_mid[0], factor[0, 768:1024, :])
    return total.astype(BF16)


def right_kernel(pos, w_own, w_pair, w_mid, factor, out):
    out[...] = right_product(w_own, w_pair, w_mid, factor)


def left_product(pos, parts, right, out, pack, full):
    x, y = pos[0], pos[1]
    for d, part in enumerate(parts):
        for e in range(4):
            at = (y + 4 - d) % 4 * 64 + (x + 4 - e) % 4 * 16
            pack[pl.ds(pl.multiple_of(at, 16), 16), :] = part[16 * e:16 * e + 16, :]
    for b in range(3):
        def piece(i):
            s = 10 * b + i
            return pack[s // 15 * SUB:(s // 15 + 1) * SUB, s % 15 * SUB:(s % 15 + 1) * SUB].astype(F32)

        unpack(piece, full.at[b])
        at = b * BLK
        out[0, at:at + BLK, :] = nn_dot(invert(full.at[b]), right[at:at + BLK, :]).astype(BF16)


def left_kernel(pos, p0, p1, p2, p3, right, out, pack, full):
    left_product(pos, (p0, p1, p2, p3), right, out, pack, full)


def last_kernel(pos, p0, p1, p2, p3, w_own, w_pair, w_mid, factor, before, out, pack, full, right):
    right[...] = right_product(w_own, w_pair, w_mid, factor)
    left_product(pos, (p0, p1, p2, p3), right, out, pack, full)


def call(kernel, pos, operands, in_specs, out_shape, scratch, out_specs=None, aliases={}):
    return pl.pallas_call(
        kernel,
        grid_spec=pltpu.PrefetchScalarGridSpec(
            num_scalar_prefetch=1,
            grid=(1,),
            in_specs=in_specs,
            out_specs=out_specs or [whole(s) for s in out_shape],
            scratch_shapes=scratch,
        ),
        out_shape=out_shape,
        input_output_aliases=aliases,
        compiler_params=pltpu.CompilerParams(vmem_limit_bytes=24 * 1024 * 1024),
        cost_estimate=pl.CostEstimate(flops=0, bytes_accessed=0, transcendentals=0),
    )(pos, *operands)


ANYWHERE = pl.BlockSpec(memory_space=pl.ANY)
ONCE = pl.Buffered(1)


def whole(a):
    return pl.BlockSpec(a.shape, lambda i, p, n=len(a.shape): (0,) * n, pipeline_mode=ONCE)


def of_layer(a, layer):
    return pl.BlockSpec((1,) + a.shape[1:], lambda i, p: (layer, 0, 0), pipeline_mode=ONCE)


def shape(*dims):
    return jax.ShapeDtypeStruct(dims, BF16)


def add(parts):
    return sum(p.astype(F32) for p in parts)


def spread(parts, axis):
    return [parts[0]] + [lax.ppermute(parts[d], axis, [(i, (i + d) % 4) for i in range(4)]) for d in (1, 2, 3)]


def chunk(a, index, rows):
    return lax.dynamic_slice_in_dim(a, index % 4 * rows, rows, 0)


def paired(w):
    return lax.ppermute(w, "x", [(0, 1), (1, 0), (2, 3), (3, 2)])


def body(acts, grads_out, weight_grad):
    y, x, zh, zl, c = (lax.axis_index(n) for n in ("y", "x", "zh", "zl", "c"))
    pos = jnp.stack([x, y, c, zh % 2 * 4 + zl * 2 + c, zh // 2, zl]).astype(jnp.int32)
    rows, width = weight_grad.shape[1:]
    barrier = lax.optimization_barrier

    covs = call(
        cov_kernel, pos, (grads_out,), [whole(grads_out)],
        [shape(128, LANES)] * 4, [VMEM((2, 256, LANES), BF16)],
    )
    covs = list(covs)
    covs[0], acts, w_ready = barrier((covs[0], acts, weight_grad))
    quarter = add(spread(covs, "y")).astype(BF16)

    whole0, whole1, mid = call(
        columns_kernel, pos, (w_ready,), [ANYWHERE], [shape(rows, width), shape(rows, width), shape(2, rows, 256)],
        [pltpu.SemaphoreType.DMA((3,))], out_specs=[ANYWHERE] * 3,
    )
    pair0, mid = paired(whole0), lax.ppermute(mid, "x", [(1, 2), (2, 1)])

    side = call(
        side_kernel, pos, (acts,),
        [pl.BlockSpec((1,) + acts.shape[1:], lambda i, p: (p[4], 0, 0), pipeline_mode=ONCE)],
        [shape(128, LANES)], [],
    )[0]
    side = lax.all_to_all(side, "y", 0, 0, tiled=True)
    side = add([side[32 * d:32 * (d + 1)] for d in range(4)]).astype(BF16)

    quarter, side, pair0, mid = barrier((quarter, side, pair0, mid))
    sends = [
        jnp.concatenate([chunk(quarter[:64], x + d, 16), chunk(quarter[64:], x + d, 16), side], axis=0)
        for d in range(4)
    ]
    both = add(spread(sends, "x")) * (1.0 / TOKENS)
    side = jnp.concatenate([both[32:48], both[48:64]], axis=1)
    side = lax.dynamic_slice_in_dim(side, x // 2 * 1280, 2560, 1).astype(BF16)

    quarter = spread([both[:32].astype(BF16)] * 4, "x")
    first, second = (jnp.concatenate([q[16 * n:16 * n + 16] for q in quarter], axis=0) for n in range(2))
    side = jnp.concatenate([side, lax.ppermute(side, "zl", [(0, 1), (1, 0)])], axis=0)
    first, second, side, whole1 = barrier((first, second, side, whole1))
    pair1 = paired(whole1)
    first = spread([first] * 4, "y")
    mine = lax.all_to_all(jnp.tile(side, (4, 1)), "zh", 0, 0, tiled=True)
    first, second, mine = barrier((first, second, mine))
    second = spread([second] * 4, "y")
    other = lax.ppermute(mine, "c", [(0, 1), (1, 0)])
    factor = call(
        factor_kernel, pos, (mine, other), [whole(mine), whole(other)], [shape(2, 1024, 384)],
        [VMEM((2, SUB, 2560), BF16), VMEM((2, 2, BLK, BLK), F32), VMEM((2, 1024, 1024), BF16)],
    )[0]

    def products(layer, w_pair):
        specs = [of_layer(weight_grad, layer), whole(w_pair), of_layer(mid, layer), of_layer(factor, layer)]
        return (weight_grad, w_pair, mid, factor), specs

    out = shape(*weight_grad.shape)
    scratch = [VMEM((256, LANES), BF16), VMEM((3, BLK, BLK), F32)]
    operands, specs = products(0, pair0)
    right = call(right_kernel, pos, operands, specs, [shape(rows, width)], [])[0]
    operands = (*first, right)
    before = call(
        left_kernel, pos, operands, [whole(a) for a in operands], [out], scratch, out_specs=[of_layer(out, 0)]
    )[0]
    operands, specs = products(1, pair1)
    return call(
        last_kernel, pos, (*second, *operands, before), [whole(a) for a in second] + specs + [ANYWHERE], [out],
        scratch + [VMEM((rows, width), BF16)], out_specs=[of_layer(out, 1)], aliases={9: 0},
    )[0]


def solution(mesh):
    fine = Mesh(mesh.devices.reshape(4, 4, 4, 2, 2), ("y", "x", "zh", "zl", "c"))
    dp, owner = ("y", "x"), ("zh", "zl", "c")
    in_specs = (P(None, dp, None), P(None, dp, owner), P(None, owner, dp))
    out_specs = P(None, owner, dp)
    return jax.shard_map(body, mesh=fine, in_specs=in_specs, out_specs=out_specs, check_vma=False)
```

```python
import jax
import jax.numpy as jnp
from jax import lax
from jax.experimental import pallas as pl
from jax.experimental.pallas import tpu as pltpu
from jax.sharding import Mesh, PartitionSpec as P

BLK = 512
SUB = 128
damping = 0.1
TOKENS = 4096
F32 = jnp.float32
BF16 = jnp.bfloat16
VMEM = pltpu.VMEM

PAIRS = [(r, c) for r in range(4) for c in range(r, 4)]
LANES = 15 * SUB


def tn_dot(a, b):
    return lax.dot_general(a, b, (((0,), (0,)), ((), ())), preferred_element_type=F32)


def nn_dot(a, b):
    return lax.dot_general(a, b, (((1,), (0,)), ((), ())), preferred_element_type=F32)


def cov_kernel(pos, acts, grads, w, h0, h1, h2, h3, early, late, mid, pack, sems):
    x, y, part = pos[0], pos[1], pos[3]
    columns = pl.ds(pl.multiple_of(jnp.where(x == 1, SUB, 0), SUB), 256)
    full = w.shape[1]
    copies = [
        pltpu.make_async_copy(w.at[:, :, columns], mid, sems.at[0]),
        pltpu.make_async_copy(w.at[0], early.at[pl.ds(0, full)], sems.at[1]),
        pltpu.make_async_copy(w.at[1, pl.ds(0, BLK)], early.at[pl.ds(full, BLK)], sems.at[2]),
        pltpu.make_async_copy(w.at[1, pl.ds(BLK, full - BLK)], late, sems.at[3]),
    ]
    for copy in copies:
        copy.start()
    sends = (h0, h1, h2, h3)
    for layer in range(2):
        for b in range(3):
            rows = grads[layer, :, b * BLK:(b + 1) * BLK]
            top = tn_dot(rows[:, :256], rows).astype(BF16)
            low = tn_dot(rows[:, 256:], rows[:, 256:]).astype(BF16)
            for i, (r, c) in enumerate(PAIRS):
                s = 10 * b + i
                if r < 2:
                    piece = top[r * SUB:(r + 1) * SUB, c * SUB:(c + 1) * SUB]
                else:
                    piece = low[(r - 2) * SUB:(r - 1) * SUB, (c - 2) * SUB:(c - 1) * SUB]
                pack[layer, s // 15 * SUB:(s // 15 + 1) * SUB, s % 15 * SUB:(s % 15 + 1) * SUB] = piece
    for d, send in enumerate(sends):
        at = pl.multiple_of((y + d) % 4 * 64, 64)
        send[0:64, :] = pack[0, pl.ds(at, 64), :]
        send[64:128, :] = pack[1, pl.ds(at, 64), :]
    k = lax.broadcasted_iota(jnp.int32, (BLK, 64), 0)
    m = lax.broadcasted_iota(jnp.int32, (BLK, 64), 1)
    select = jnp.where(k == m // 16 * SUB + part * 16 + m % 16, 1.0, 0.0).astype(BF16)
    for d, send in enumerate(sends):
        start = (y + d) % 4 * (3 * BLK)
        for b in range(3):
            rows = acts[0, :, pl.ds(pl.multiple_of(start + b * BLK, BLK), BLK)]
            chosen = nn_dot(rows, select).astype(BF16)
            cov = tn_dot(chosen, rows).astype(BF16)
            for i, (r, c) in enumerate(PAIRS):
                s = 10 * b + i
                at = 128 + s // 15 * 16
                send[at:at + 16, s % 15 * SUB:(s % 15 + 1) * SUB] = cov[r * 16:(r + 1) * 16, c * SUB:(c + 1) * SUB]
    for copy in copies:
        copy.wait()


def unpack(piece, full):
    for i, (r, c) in enumerate(PAIRS):
        tile = piece(i)
        full[r * SUB:(r + 1) * SUB, c * SUB:(c + 1) * SUB] = tile.astype(full.dtype)
        if r != c:
            full[c * SUB:(c + 1) * SUB, r * SUB:(r + 1) * SUB] = tile.T.astype(full.dtype)


def invert(full):
    ri = lax.broadcasted_iota(jnp.int32, (BLK, BLK), 0)
    ci = lax.broadcasted_iota(jnp.int32, (BLK, BLK), 1)
    diagonal = ri == ci
    matrix = full[...] + jnp.where(diagonal, damping, 0.0)
    two_eye = jnp.where(diagonal, 2.0, 0.0)
    sums = jnp.sum(jnp.abs(matrix), axis=0, keepdims=True)
    alpha = (1.0 / jnp.max(sums, axis=1, keepdims=True)).astype(BF16).astype(F32)
    low = matrix.astype(BF16)
    residue = (two_eye - low.astype(F32) * alpha).astype(BF16)
    iterate = (residue.astype(F32) * alpha).astype(BF16)
    image = nn_dot(low, iterate)
    residue = (two_eye - image).astype(BF16)
    return nn_dot(iterate, residue).astype(BF16)


OFFSETS = (0, -1, 1, -2, 2, -3, 3, -4)


def factor_kernel(pos, mine, other, out, pack, full, diag):
    x, core, z = pos[0], pos[2], pos[5]
    for n, offset in enumerate(OFFSETS):
        rows = slice(16 * n, 16 * n + 16)
        at = (z + 8 + offset) % 8 * 32
        pack[pl.ds(pl.multiple_of(at + core * 16, 16), 16), :] = mine[rows, :]
        pack[pl.ds(pl.multiple_of(at + 16 - core * 16, 16), 16), :] = other[rows, :]
    base = x // 2 * BLK
    own = pl.multiple_of(x * 384 - base, SUB)
    pair = pl.multiple_of((x + 1 - 2 * (x % 2)) * 384 - base, SUB)
    mid = pl.multiple_of(jnp.where(x == 1, 768, 0), SUB)
    columns = pl.ds(own, 384)
    for layer in range(2):
        for b in range(2):
            at = b * BLK
            unpack(
                lambda i: pack[layer * SUB:(layer + 1) * SUB, b * 1280 + i * SUB:b * 1280 + (i + 1) * SUB].astype(F32),
                full.at[layer, b],
            )
            diag[layer, at:at + BLK, at:at + BLK] = invert(full.at[layer, b])
            diag[layer, at:at + BLK, BLK - at:2 * BLK - at] = jnp.zeros((BLK, BLK), BF16)
        out[layer, 0:384, :] = diag[layer, pl.ds(own, 384), columns]
        out[layer, 384:768, :] = diag[layer, pl.ds(pair, 384), columns]
        out[layer, 768:1024, :] = diag[layer, pl.ds(mid, 256), columns]


def right_kernel(pos, w_own, w_mid, factor, *refs):
    out, at = refs[-1], 0
    for pair in refs[:-1]:
        rows = slice(at, at + pair.shape[0])
        total = nn_dot(w_own[0, rows, :], factor[0, 0:384, :])
        total += nn_dot(pair[...], factor[0, 384:768, :])
        total += nn_dot(w_mid[0, rows, :], factor[0, 768:1024, :])
        out[rows, :] = total.astype(BF16)
        at += pair.shape[0]


def left_kernel(pos, gathered, r0, r1, out, pack, full, ready, sems):
    copies = []
    for layer, right in enumerate((r0, r1)):
        for k in range(16):
            rows = 32 * k + 16 * layer
            pack[layer, 16 * k:16 * k + 16, :] = gathered[rows:rows + 16, :]
        for b in range(3):
            def piece(i):
                s = 10 * b + i
                return pack[layer, s // 15 * SUB:(s // 15 + 1) * SUB, s % 15 * SUB:(s % 15 + 1) * SUB].astype(F32)

            unpack(piece, full.at[layer, b])
            at = b * BLK
            n = 3 * layer + b
            ready[n] = nn_dot(invert(full.at[layer, b]), right[at:at + BLK, :]).astype(BF16)
            copies.append(pltpu.make_async_copy(ready.at[n], out.at[layer, pl.ds(at, BLK)], sems.at[n]))
            copies[-1].start()
    for copy in copies:
        copy.wait()


def call(kernel, pos, operands, in_specs, out_shape, scratch, out_specs=None, aliases={}):
    return pl.pallas_call(
        kernel,
        grid_spec=pltpu.PrefetchScalarGridSpec(
            num_scalar_prefetch=1,
            grid=(1,),
            in_specs=in_specs,
            out_specs=out_specs or [whole(s) for s in out_shape],
            scratch_shapes=scratch,
        ),
        out_shape=out_shape,
        input_output_aliases=aliases,
        compiler_params=pltpu.CompilerParams(vmem_limit_bytes=56 * 1024 * 1024),
        cost_estimate=pl.CostEstimate(flops=0, bytes_accessed=0, transcendentals=0),
    )(pos, *operands)


ANYWHERE = pl.BlockSpec(memory_space=pl.ANY)
ONCE = pl.Buffered(1)


def whole(a):
    return pl.BlockSpec(a.shape, lambda i, p, n=len(a.shape): (0,) * n, pipeline_mode=ONCE)


def of_layer(a, layer):
    return pl.BlockSpec((1,) + a.shape[1:], lambda i, p: (layer, 0, 0), pipeline_mode=ONCE)


def shape(*dims):
    return jax.ShapeDtypeStruct(dims, BF16)


def add(parts):
    return sum(p.astype(F32) for p in parts)


def spread(parts, axis):
    return [parts[0]] + [lax.ppermute(parts[d], axis, [(i, (i + d) % 4) for i in range(4)]) for d in (1, 2, 3)]


def chunk(a, index, rows):
    return lax.dynamic_slice_in_dim(a, index % 4 * rows, rows, 0)


def paired(w):
    return lax.ppermute(w, "x", [(0, 1), (1, 0), (2, 3), (3, 2)])


def body(acts, grads_out, weight_grad):
    y, x, z, c = (lax.axis_index(n) for n in ("y", "x", "z", "c"))
    pos = jnp.stack([x, y, c, z % 4 * 2 + c, z // 4, z]).astype(jnp.int32)
    rows, width = weight_grad.shape[1:]
    barrier = lax.optimization_barrier

    covs = call(
        cov_kernel, pos, (acts, grads_out, weight_grad),
        [
            pl.BlockSpec((1,) + acts.shape[1:], lambda i, p: (p[4], 0, 0), pipeline_mode=ONCE),
            whole(grads_out), ANYWHERE,
        ],
        [shape(160, LANES)] * 4 + [shape(rows + BLK, width), shape(rows - BLK, width), shape(2, rows, 256)],
        [VMEM((2, 256, LANES), BF16), pltpu.SemaphoreType.DMA((4,))],
        out_specs=[whole(shape(160, LANES))] * 4 + [ANYWHERE] * 3,
    )
    early, late, mid = covs[4:]
    early, mid = paired(early), lax.ppermute(mid, "x", [(1, 2), (2, 1)])

    quarter = add(spread(covs[:4], "y")).astype(BF16)
    quarter, early, mid = barrier((quarter, early, mid))
    sends = [
        jnp.concatenate([chunk(quarter[:64], x + d, 16), chunk(quarter[64:128], x + d, 16), quarter[128:]], axis=0)
        for d in range(4)
    ]
    both = add(spread(sends, "x")) * (1.0 / TOKENS)
    side = jnp.concatenate([both[32:48], both[48:64]], axis=1)
    side = lax.dynamic_slice_in_dim(side, x // 2 * 1280, 2560, 1).astype(BF16)
    own, side, late = barrier((both[:32].astype(BF16), side, late))

    gathered = lax.all_to_all(jnp.tile(own, (16, 1)), ("y", "x"), 0, 0, tiled=True)
    late = paired(late)
    up = down = side
    mine = [side]
    for step in range(1, 5):
        up = lax.ppermute(up, "z", [(i, (i + 1) % 8) for i in range(8)])
        mine.append(up)
        if step < 4:
            down = lax.ppermute(down, "z", [(i, (i + 7) % 8) for i in range(8)])
            mine.append(down)
    mine = jnp.concatenate(mine, axis=0)
    other = lax.ppermute(mine, "c", [(0, 1), (1, 0)])
    factor = call(
        factor_kernel, pos, (mine, other), [whole(mine), whole(other)], [shape(2, 1024, 384)],
        [VMEM((256, 2560), BF16), VMEM((2, 2, BLK, BLK), F32), VMEM((2, 1024, 1024), BF16)],
    )[0]
    rights = []
    for layer in range(2):
        if layer == 0:
            pairs = [(early, pl.BlockSpec((rows, width), lambda i, p: (0, 0), pipeline_mode=ONCE))]
        else:
            block = rows // BLK
            pairs = [
                (early, pl.BlockSpec((BLK, width), lambda i, p: (block, 0), pipeline_mode=ONCE)),
                (late, whole(late)),
            ]
        rights.append(call(
            right_kernel, pos, (weight_grad, mid, factor, *(p[0] for p in pairs)),
            [of_layer(weight_grad, layer), of_layer(mid, layer), of_layer(factor, layer), *(p[1] for p in pairs)],
            [shape(rows, width)], [],
        )[0])
    return call(
        left_kernel, pos, (gathered, *rights), [whole(gathered), whole(rights[0]), whole(rights[1])],
        [shape(*weight_grad.shape)],
        [
            VMEM((2, 256, LANES), BF16), VMEM((2, 3, BLK, BLK), F32), VMEM((6, BLK, width), BF16),
            pltpu.SemaphoreType.DMA((6,)),
        ],
        out_specs=[ANYWHERE],
    )[0]


def solution(mesh):
    fine = Mesh(mesh.devices.reshape(4, 4, 8, 2), ("y", "x", "z", "c"))
    dp, owner = ("y", "x"), ("z", "c")
    in_specs = (P(None, dp, None), P(None, dp, owner), P(None, owner, dp))
    out_specs = P(None, owner, dp)
    return jax.shard_map(body, mesh=fine, in_specs=in_specs, out_specs=out_specs, check_vma=False)
```

```python
import jax
import jax.numpy as jnp
from jax import lax
from jax.experimental import pallas as pl
from jax.experimental.pallas import tpu as pltpu
from jax.sharding import Mesh, PartitionSpec as P

BLK = 512
SUB = 128
damping = 0.1
TOKENS = 4096
F32 = jnp.float32
BF16 = jnp.bfloat16
VMEM = pltpu.VMEM

PAIRS = [(r, c) for r in range(4) for c in range(r, 4)]
LANES = 15 * SUB


def tn_dot(a, b):
    return lax.dot_general(a, b, (((0,), (0,)), ((), ())), preferred_element_type=F32)


def nn_dot(a, b):
    return lax.dot_general(a, b, (((1,), (0,)), ((), ())), preferred_element_type=F32)


def relay(copies, sems):
    loads = [pltpu.make_async_copy(a, b, sems.at[0, n]) for n, (a, b, _) in enumerate(copies)]
    stores = [pltpu.make_async_copy(b, c, sems.at[1, n]) for n, (_, b, c) in enumerate(copies)]
    for load in loads:
        load.start()
    for load, store in zip(loads, stores):
        load.wait()
        store.start()
    for store in stores:
        store.wait()


def middle(pos):
    return pl.ds(pl.multiple_of(jnp.where(pos[0] == 1, SUB, 0), SUB), 256)


def early_kernel(pos, w, whole0, mid0, held, held_mid, sems):
    full, rest = w.shape[1], w.shape[1] - BLK
    relay([
        (w.at[0], held, whole0),
        (w.at[0, :, middle(pos)], held_mid.at[pl.ds(0, full)], mid0.at[pl.ds(0, full)]),
        (w.at[1, pl.ds(0, rest), middle(pos)], held_mid.at[pl.ds(full, rest)], mid0.at[pl.ds(full, rest)]),
    ], sems)


def late_kernel(pos, w, whole1, mid1, held, held_mid, sems):
    rest = w.shape[1] - BLK
    relay([(w.at[1], held, whole1), (w.at[1, pl.ds(rest, BLK), middle(pos)], held_mid, mid1)], sems)


def cov_kernel(pos, grads, h0, h1, h2, h3, pack):
    y = pos[1]
    for layer in range(2):
        for b in range(3):
            rows = grads[layer, :, b * BLK:(b + 1) * BLK]
            top = tn_dot(rows[:, :256], rows).astype(BF16)
            low = tn_dot(rows[:, 256:], rows[:, 256:]).astype(BF16)
            for i, (r, c) in enumerate(PAIRS):
                s = 10 * b + i
                if r < 2:
                    piece = top[r * SUB:(r + 1) * SUB, c * SUB:(c + 1) * SUB]
                else:
                    piece = low[(r - 2) * SUB:(r - 1) * SUB, (c - 2) * SUB:(c - 1) * SUB]
                pack[layer, s // 15 * SUB:(s // 15 + 1) * SUB, s % 15 * SUB:(s % 15 + 1) * SUB] = piece
    for d, send in enumerate((h0, h1, h2, h3)):
        at = pl.multiple_of((y + d) % 4 * 64, 64)
        send[0:64, :] = pack[0, pl.ds(at, 64), :]
        send[64:128, :] = pack[1, pl.ds(at, 64), :]


def side_kernel(pos, acts, out):
    part = pos[3]
    k = lax.broadcasted_iota(jnp.int32, (BLK, 64), 0)
    m = lax.broadcasted_iota(jnp.int32, (BLK, 64), 1)
    select = jnp.where(k == m // 16 * SUB + part * 16 + m % 16, 1.0, 0.0).astype(BF16)
    for b in range(3):
        rows = acts[0, :, b * BLK:(b + 1) * BLK]
        chosen = nn_dot(rows, select).astype(BF16)
        cov = tn_dot(chosen, rows).astype(BF16)
        for i, (r, c) in enumerate(PAIRS):
            s = 10 * b + i
            at = s // 15 * 16
            out[at:at + 16, s % 15 * SUB:(s % 15 + 1) * SUB] = cov[r * 16:(r + 1) * 16, c * SUB:(c + 1) * SUB]


def total_kernel(pos, parts, out):
    total = (parts[0:32, :].astype(F32) + parts[32:64, :].astype(F32)) + (
        parts[64:96, :].astype(F32) + parts[96:128, :].astype(F32)
    )
    for n in range(4):
        out[32 * n:32 * n + 32, :] = total.astype(BF16)


def chosen_kernel(pos, parts, out):
    x = pos[0]
    total = ((parts[0:32, :].astype(F32) + parts[32:64, :].astype(F32)) + (
        parts[64:96, :].astype(F32) + parts[96:128, :].astype(F32)
    )) * (1.0 / TOKENS)
    upper, lower = total[0:16, :].astype(BF16), total[16:32, :].astype(BF16)

    @pl.when(x < 2)
    def _():
        for n in range(8):
            out[16 * n:16 * n + 16, 0:LANES] = upper
            out[16 * n:16 * n + 16, LANES:2560] = lower[:, 0:640]

    @pl.when(x >= 2)
    def _():
        for n in range(8):
            out[16 * n:16 * n + 16, 0:640] = upper[:, 1280:LANES]
            out[16 * n:16 * n + 16, 640:2560] = lower


def unpack(piece, full):
    for i, (r, c) in enumerate(PAIRS):
        tile = piece(i)
        full[r * SUB:(r + 1) * SUB, c * SUB:(c + 1) * SUB] = tile.astype(full.dtype)
        if r != c:
            full[c * SUB:(c + 1) * SUB, r * SUB:(r + 1) * SUB] = tile.T.astype(full.dtype)


def invert(full):
    ri = lax.broadcasted_iota(jnp.int32, (BLK, BLK), 0)
    ci = lax.broadcasted_iota(jnp.int32, (BLK, BLK), 1)
    diagonal = ri == ci
    matrix = full[...] + jnp.where(diagonal, damping, 0.0)
    two_eye = jnp.where(diagonal, 2.0, 0.0)
    sums = jnp.sum(jnp.abs(matrix), axis=0, keepdims=True)
    alpha = (1.0 / jnp.max(sums, axis=1, keepdims=True)).astype(BF16).astype(F32)
    low = matrix.astype(BF16)
    residue = (two_eye - low.astype(F32) * alpha).astype(BF16)
    iterate = (residue.astype(F32) * alpha).astype(BF16)
    image = nn_dot(low, iterate)
    residue = (two_eye - image).astype(BF16)
    return nn_dot(iterate, residue).astype(BF16)


def twice_kernel(pos, a, out):
    out[0:128, :] = a[...]
    out[128:256, :] = a[...]


def factor_kernel(pos, both, out, pack, full, diag):
    x = pos[0]
    for z in range(8):
        for core in range(2):
            rows = 128 * core + 16 * z
            pack[32 * z + 16 * core:32 * z + 16 * core + 16, :] = both[rows:rows + 16, :]
    base = x // 2 * BLK
    own = pl.multiple_of(x * 384 - base, SUB)
    pair = pl.multiple_of((x + 1 - 2 * (x % 2)) * 384 - base, SUB)
    mid = pl.multiple_of(jnp.where(x == 1, 768, 0), SUB)
    columns = pl.ds(own, 384)
    for layer in range(2):
        for b in range(2):
            at = b * BLK
            unpack(
                lambda i: pack[layer * SUB:(layer + 1) * SUB, b * 1280 + i * SUB:b * 1280 + (i + 1) * SUB].astype(F32),
                full.at[layer, b],
            )
            diag[layer, at:at + BLK, at:at + BLK] = invert(full.at[layer, b])
            diag[layer, at:at + BLK, BLK - at:2 * BLK - at] = jnp.zeros((BLK, BLK), BF16)
        out[layer, 0:384, :] = diag[layer, pl.ds(own, 384), columns]
        out[layer, 384:768, :] = diag[layer, pl.ds(pair, 384), columns]
        out[layer, 768:1024, :] = diag[layer, pl.ds(mid, 256), columns]


def right_kernel(pos, w_own, w_pair, factor, *refs):
    out, at = refs[-1], 0
    for mid in refs[:-1]:
        rows = slice(at, at + mid.shape[0])
        total = nn_dot(w_own[0, rows, :], factor[0, 0:384, :])
        total += nn_dot(w_pair[rows, :], factor[0, 384:768, :])
        total += nn_dot(mid[...], factor[0, 768:1024, :])
        out[rows, :] = total.astype(BF16)
        at += mid.shape[0]


def left_kernel(pos, p0, p1, p2, p3, r0, r1, out, pack, full, ready, sems):
    x, y = pos[0], pos[1]
    copies = []
    for layer, right in enumerate((r0, r1)):
        for d, part in enumerate((p0, p1, p2, p3)):
            for e in range(4):
                at = (y + 4 - d) % 4 * 64 + (x + 4 - e) % 4 * 16
                rows = 32 * e + 16 * layer
                pack[layer, pl.ds(pl.multiple_of(at, 16), 16), :] = part[rows:rows + 16, :]
        for b in range(3):
            def piece(i):
                s = 10 * b + i
                return pack[layer, s // 15 * SUB:(s // 15 + 1) * SUB, s % 15 * SUB:(s % 15 + 1) * SUB].astype(F32)

            unpack(piece, full.at[layer, b])
            at = b * BLK
            n = 3 * layer + b
            ready[n] = nn_dot(invert(full.at[layer, b]), right[at:at + BLK, :]).astype(BF16)
            copies.append(pltpu.make_async_copy(ready.at[n], out.at[layer, pl.ds(at, BLK)], sems.at[n]))
            copies[-1].start()
    for copy in copies:
        copy.wait()


def call(kernel, pos, operands, in_specs, out_shape, scratch, out_specs=None, vmem=40, flops=0, grid=1):
    return pl.pallas_call(
        kernel,
        grid_spec=pltpu.PrefetchScalarGridSpec(
            num_scalar_prefetch=1,
            grid=(grid,),
            in_specs=in_specs,
            out_specs=out_specs or [whole(s) for s in out_shape],
            scratch_shapes=scratch,
        ),
        out_shape=out_shape,
        compiler_params=pltpu.CompilerParams(vmem_limit_bytes=vmem * 1024 * 1024),
        cost_estimate=pl.CostEstimate(flops=flops, bytes_accessed=0, transcendentals=0),
    )(pos, *operands)


ANYWHERE = pl.BlockSpec(memory_space=pl.ANY)
ONCE = pl.Buffered(1)


def whole(a):
    return pl.BlockSpec(a.shape, lambda i, p, n=len(a.shape): (0,) * n, pipeline_mode=ONCE)


def of_layer(a, layer):
    return pl.BlockSpec((1,) + a.shape[1:], lambda i, p: (layer, 0, 0), pipeline_mode=ONCE)


def part(rows, n):
    return pl.BlockSpec((rows, 256), lambda i, p: (n, 0), pipeline_mode=ONCE)


def shape(*dims):
    return jax.ShapeDtypeStruct(dims, BF16)


def add(parts):
    return sum(p.astype(F32) for p in parts)


def spread(parts, axis):
    return [parts[0]] + [lax.ppermute(parts[d], axis, [(i, (i + d) % 4) for i in range(4)]) for d in (1, 2, 3)]


def chunk(a, index, rows):
    return lax.dynamic_slice_in_dim(a, index % 4 * rows, rows, 0)


def exchange(w, middle):
    pair = lax.ppermute(w, "x", [(0, 1), (1, 0), (2, 3), (3, 2)])
    return [pair, lax.ppermute(middle, "x", [(1, 2), (2, 1)])]


def body(acts, grads_out, weight_grad):
    y, x, z, c = (lax.axis_index(n) for n in ("y", "x", "z", "c"))
    pos = jnp.stack([x, y, c, z % 4 * 2 + c, z // 4, z]).astype(jnp.int32)
    rows, width = weight_grad.shape[1:]
    barrier = lax.optimization_barrier

    def relayed(kernel, w, *shapes, **options):
        return call(
            kernel, pos, (w,), [ANYWHERE], list(shapes),
            [VMEM(a.shape, BF16) for a in shapes] + [pltpu.SemaphoreType.DMA((2, 3))],
            out_specs=[ANYWHERE] * 2, vmem=60, **options,
        )

    w_early = exchange(*relayed(early_kernel, weight_grad, shape(rows, width), shape(2 * rows - BLK, 256)))

    def blocks(operands):
        pos, acts, grads_out, weight_grad = operands
        side = call(
            side_kernel, pos, (acts,),
            [pl.BlockSpec((1, acts.shape[1], 3 * BLK), lambda i, p: (p[4], 0, i))],
            [shape(128, LANES)], [], out_specs=[pl.BlockSpec((32, LANES), lambda i, p: (i, 0))], vmem=60, grid=4,
        )[0]
        covs = call(
            cov_kernel, pos, (grads_out,), [whole(grads_out)], [shape(128, LANES)] * 4,
            [VMEM((2, 256, LANES), BF16)], vmem=60, flops=10_000_000_000,
        )
        w_late = relayed(late_kernel, weight_grad, shape(rows, width), shape(BLK, 256), flops=5_000_000_000)
        return lax.all_to_all(side, "y", 0, 0, tiled=True), *w_late, *covs

    always = x + y + z + c < 64
    late = (rows, width), (BLK, 256)
    side, *covs = lax.cond(
        always, blocks, lambda operands: tuple(jnp.zeros(n, BF16) for n in ((128, LANES), *late, *((128, LANES),) * 4)),
        (pos, acts, grads_out, weight_grad),
    )
    w_late, covs = covs[:2], covs[2:]
    covs = spread(covs, "y")

    def sum_side(operands):
        pos, side, _ = operands
        side = call(total_kernel, pos, (side,), [whole(side)], [shape(128, LANES)], [])[0]
        side = lax.all_to_all(side, "x", 0, 0, tiled=True)
        return call(chosen_kernel, pos, (side,), [whole(side)], [shape(128, 2560)], [])[0]

    side = lax.cond(always, sum_side, lambda operands: jnp.zeros((128, 2560), BF16), (pos, side, covs[0]))
    mine = lax.all_to_all(side, "z", 0, 0, tiled=True)
    *covs, _ = barrier((*covs, side))
    quarter = add(covs).astype(BF16)
    quarter, w_early = barrier((quarter, w_early))

    sends = [
        jnp.concatenate([chunk(quarter[:64], x + d, 16), chunk(quarter[64:], x + d, 16)], axis=0) for d in range(4)
    ]
    own = (add(spread(sends, "x")) * (1.0 / TOKENS)).astype(BF16)
    quarter = jnp.concatenate(spread([own] * 4, "x"), axis=0)
    quarter, w_late = barrier((quarter, w_late))
    w_late = exchange(*w_late)
    parts = spread([quarter] * 4, "y")

    twice = call(twice_kernel, pos, (mine,), [whole(mine)], [shape(256, 2560)], [], flops=60_000_000_000)[0]

    def invert_side(operands):
        pos, twice, _ = operands
        both = lax.all_to_all(twice, "c", 0, 0, tiled=True)
        return call(
            factor_kernel, pos, (both,), [whole(both)], [shape(2, 1024, 384)],
            [VMEM((256, 2560), BF16), VMEM((2, 2, BLK, BLK), F32), VMEM((2, 1024, 1024), BF16)],
        )[0]

    factor = lax.cond(
        always, invert_side, lambda operands: jnp.zeros((2, 1024, 384), BF16), (pos, twice, parts[0])
    )
    block = rows // BLK
    rights = []
    for layer, pair in enumerate((w_early[0], w_late[0])):
        mids = [(w_early[1], part(rows, 0))] if layer == 0 else [
            (w_early[1], part(BLK, n)) for n in range(block, 2 * block - 1)
        ] + [(w_late[1], whole(w_late[1]))]
        rights.append(call(
            right_kernel, pos, (weight_grad, pair, factor, *(m[0] for m in mids)),
            [of_layer(weight_grad, layer), whole(pair), of_layer(factor, layer), *(m[1] for m in mids)],
            [shape(rows, width)], [],
        )[0])
    return call(
        left_kernel, pos, (*parts, *rights), [whole(a) for a in (*parts, *rights)],
        [shape(*weight_grad.shape)],
        [
            VMEM((2, 256, LANES), BF16), VMEM((2, 3, BLK, BLK), F32), VMEM((6, BLK, width), BF16),
            pltpu.SemaphoreType.DMA((6,)),
        ],
        out_specs=[ANYWHERE],
    )[0]


def solution(mesh):
    fine = Mesh(mesh.devices.reshape(4, 4, 8, 2), ("y", "x", "z", "c"))
    dp, owner = ("y", "x"), ("z", "c")
    in_specs = (P(None, dp, None), P(None, dp, owner), P(None, owner, dp))
    out_specs = P(None, owner, dp)
    return jax.shard_map(body, mesh=fine, in_specs=in_specs, out_specs=out_specs, check_vma=False)
```

```python
import jax
import jax.numpy as jnp
from jax import lax
from jax.experimental import pallas as pl
from jax.experimental.pallas import tpu as pltpu
from jax.sharding import Mesh, PartitionSpec as P

BLK = 512
SUB = 128
damping = 0.1
TOKENS = 4096
F32 = jnp.float32
BF16 = jnp.bfloat16
VMEM = pltpu.VMEM

PAIRS = [(r, c) for r in range(4) for c in range(r, 4)]
LANES = 15 * SUB


def tn_dot(a, b):
    return lax.dot_general(a, b, (((0,), (0,)), ((), ())), preferred_element_type=F32)


def nn_dot(a, b):
    return lax.dot_general(a, b, (((1,), (0,)), ((), ())), preferred_element_type=F32)


def middle(pos):
    return pl.ds(pl.multiple_of(jnp.where(pos[0] == 1, SUB, 0), SUB), 256)


def late_kernel(pos, w, rest, out, mid, held_rest, held, held_mid, sems):
    size = rest.shape[0]
    sources = (
        (w.at[0, pl.ds(w.shape[1] - size, size)], held_rest, rest),
        (w.at[1], held, out),
        (w.at[1, :, middle(pos)], held_mid, mid),
    )
    loads = [pltpu.make_async_copy(a, b, sems.at[0, n]) for n, (a, b, _) in enumerate(sources)]
    stores = [pltpu.make_async_copy(b, c, sems.at[1, n]) for n, (_, b, c) in enumerate(sources)]
    for load in loads:
        load.start()
    for load, store in zip(loads, stores):
        load.wait()
        store.start()
    for store in stores:
        store.wait()


def cov_kernel(pos, grads, h0, h1, h2, h3, pack):
    y = pos[1]
    for layer in range(2):
        for b in range(3):
            rows = grads[layer, :, b * BLK:(b + 1) * BLK]
            top = tn_dot(rows[:, :256], rows).astype(BF16)
            low = tn_dot(rows[:, 256:], rows[:, 256:]).astype(BF16)
            for i, (r, c) in enumerate(PAIRS):
                s = 10 * b + i
                if r < 2:
                    piece = top[r * SUB:(r + 1) * SUB, c * SUB:(c + 1) * SUB]
                else:
                    piece = low[(r - 2) * SUB:(r - 1) * SUB, (c - 2) * SUB:(c - 1) * SUB]
                pack[layer, s // 15 * SUB:(s // 15 + 1) * SUB, s % 15 * SUB:(s % 15 + 1) * SUB] = piece
    for d, send in enumerate((h0, h1, h2, h3)):
        at = pl.multiple_of((y + d) % 4 * 64, 64)
        send[0:64, :] = pack[0, pl.ds(at, 64), :]
        send[64:128, :] = pack[1, pl.ds(at, 64), :]


def side_kernel(pos, acts, w, out, early, mid, held, held_mid, sems):
    part, step = pos[3], pl.program_id(0)
    sources = (w.at[0, pl.ds(0, early.shape[0])], held, early), (w.at[0, :, middle(pos)], held_mid, mid)
    loads = [pltpu.make_async_copy(a, b, sems.at[0, n]) for n, (a, b, _) in enumerate(sources)]
    stores = [pltpu.make_async_copy(b, c, sems.at[1, n]) for n, (_, b, c) in enumerate(sources)]

    @pl.when(step == 0)
    def _():
        for load in loads:
            load.start()

    @pl.when(step == 2)
    def _():
        for load, store in zip(loads, stores):
            load.wait()
            store.start()

    k = lax.broadcasted_iota(jnp.int32, (BLK, 64), 0)
    m = lax.broadcasted_iota(jnp.int32, (BLK, 64), 1)
    select = jnp.where(k == m // 16 * SUB + part * 16 + m % 16, 1.0, 0.0).astype(BF16)
    for b in range(3):
        rows = acts[0, :, b * BLK:(b + 1) * BLK]
        chosen = nn_dot(rows, select).astype(BF16)
        cov = tn_dot(chosen, rows).astype(BF16)
        for i, (r, c) in enumerate(PAIRS):
            s = 10 * b + i
            at = s // 15 * 16
            out[at:at + 16, s % 15 * SUB:(s % 15 + 1) * SUB] = cov[r * 16:(r + 1) * 16, c * SUB:(c + 1) * SUB]

    @pl.when(step == 3)
    def _():
        for store in stores:
            store.wait()


def total_kernel(pos, parts, out):
    total = (parts[0:32, :].astype(F32) + parts[32:64, :].astype(F32)) + (
        parts[64:96, :].astype(F32) + parts[96:128, :].astype(F32)
    )
    for n in range(4):
        out[32 * n:32 * n + 32, :] = total.astype(BF16)


def chosen_kernel(pos, parts, out):
    x = pos[0]
    total = ((parts[0:32, :].astype(F32) + parts[32:64, :].astype(F32)) + (
        parts[64:96, :].astype(F32) + parts[96:128, :].astype(F32)
    )) * (1.0 / TOKENS)
    upper, lower = total[0:16, :].astype(BF16), total[16:32, :].astype(BF16)

    @pl.when(x < 2)
    def _():
        for n in range(8):
            out[16 * n:16 * n + 16, 0:LANES] = upper
            out[16 * n:16 * n + 16, LANES:2560] = lower[:, 0:640]

    @pl.when(x >= 2)
    def _():
        for n in range(8):
            out[16 * n:16 * n + 16, 0:640] = upper[:, 1280:LANES]
            out[16 * n:16 * n + 16, 640:2560] = lower


def unpack(piece, full):
    for i, (r, c) in enumerate(PAIRS):
        tile = piece(i)
        full[r * SUB:(r + 1) * SUB, c * SUB:(c + 1) * SUB] = tile.astype(full.dtype)
        if r != c:
            full[c * SUB:(c + 1) * SUB, r * SUB:(r + 1) * SUB] = tile.T.astype(full.dtype)


def invert(full):
    ri = lax.broadcasted_iota(jnp.int32, (BLK, BLK), 0)
    ci = lax.broadcasted_iota(jnp.int32, (BLK, BLK), 1)
    diagonal = ri == ci
    matrix = full[...] + jnp.where(diagonal, damping, 0.0)
    two_eye = jnp.where(diagonal, 2.0, 0.0)
    sums = jnp.sum(jnp.abs(matrix), axis=0, keepdims=True)
    alpha = (1.0 / jnp.max(sums, axis=1, keepdims=True)).astype(BF16).astype(F32)
    low = matrix.astype(BF16)
    residue = (two_eye - low.astype(F32) * alpha).astype(BF16)
    iterate = (residue.astype(F32) * alpha).astype(BF16)
    image = nn_dot(low, iterate)
    residue = (two_eye - image).astype(BF16)
    return nn_dot(iterate, residue).astype(BF16)


def factor_kernel(pos, mine, other, out, pack, full, diag):
    x, core = pos[0], pos[2]
    for z in range(8):
        rows = slice(16 * z, 16 * z + 16)
        pack[pl.ds(pl.multiple_of(32 * z + core * 16, 16), 16), :] = mine[rows, :]
        pack[pl.ds(pl.multiple_of(32 * z + 16 - core * 16, 16), 16), :] = other[rows, :]
    base = x // 2 * BLK
    own = pl.multiple_of(x * 384 - base, SUB)
    pair = pl.multiple_of((x + 1 - 2 * (x % 2)) * 384 - base, SUB)
    mid = pl.multiple_of(jnp.where(x == 1, 768, 0), SUB)
    columns = pl.ds(own, 384)
    for layer in range(2):
        for b in range(2):
            at = b * BLK
            unpack(
                lambda i: pack[layer * SUB:(layer + 1) * SUB, b * 1280 + i * SUB:b * 1280 + (i + 1) * SUB].astype(F32),
                full.at[layer, b],
            )
            diag[layer, at:at + BLK, at:at + BLK] = invert(full.at[layer, b])
            diag[layer, at:at + BLK, BLK - at:2 * BLK - at] = jnp.zeros((BLK, BLK), BF16)
        out[layer, 0:384, :] = diag[layer, pl.ds(own, 384), columns]
        out[layer, 384:768, :] = diag[layer, pl.ds(pair, 384), columns]
        out[layer, 768:1024, :] = diag[layer, pl.ds(mid, 256), columns]


def right_kernel(pos, w_own, w_mid, factor, *refs):
    out, at = refs[-1], 0
    for pair in refs[:-1]:
        rows = slice(at, at + pair.shape[0])
        total = nn_dot(w_own[0, rows, :], factor[0, 0:384, :])
        total += nn_dot(pair[...], factor[0, 384:768, :])
        total += nn_dot(w_mid[rows, :], factor[0, 768:1024, :])
        out[rows, :] = total.astype(BF16)
        at += pair.shape[0]


def left_kernel(pos, p0, p1, p2, p3, r0, r1, out, pack, full, ready, sems):
    x, y = pos[0], pos[1]
    copies = []
    for layer, right in enumerate((r0, r1)):
        for d, part in enumerate((p0, p1, p2, p3)):
            for e in range(4):
                at = (y + 4 - d) % 4 * 64 + (x + 4 - e) % 4 * 16
                rows = 32 * e + 16 * layer
                pack[layer, pl.ds(pl.multiple_of(at, 16), 16), :] = part[rows:rows + 16, :]
        for b in range(3):
            def piece(i):
                s = 10 * b + i
                return pack[layer, s // 15 * SUB:(s // 15 + 1) * SUB, s % 15 * SUB:(s % 15 + 1) * SUB].astype(F32)

            unpack(piece, full.at[layer, b])
            at = b * BLK
            n = 3 * layer + b
            ready[n] = nn_dot(invert(full.at[layer, b]), right[at:at + BLK, :]).astype(BF16)
            copies.append(pltpu.make_async_copy(ready.at[n], out.at[layer, pl.ds(at, BLK)], sems.at[n]))
            copies[-1].start()
    for copy in copies:
        copy.wait()


def call(kernel, pos, operands, in_specs, out_shape, scratch, out_specs=None, vmem=40, flops=0, grid=1):
    return pl.pallas_call(
        kernel,
        grid_spec=pltpu.PrefetchScalarGridSpec(
            num_scalar_prefetch=1,
            grid=(grid,),
            in_specs=in_specs,
            out_specs=out_specs or [whole(s) for s in out_shape],
            scratch_shapes=scratch,
        ),
        out_shape=out_shape,
        compiler_params=pltpu.CompilerParams(vmem_limit_bytes=vmem * 1024 * 1024),
        cost_estimate=pl.CostEstimate(flops=flops, bytes_accessed=0, transcendentals=0),
    )(pos, *operands)


ANYWHERE = pl.BlockSpec(memory_space=pl.ANY)
ONCE = pl.Buffered(1)


def whole(a):
    return pl.BlockSpec(a.shape, lambda i, p, n=len(a.shape): (0,) * n, pipeline_mode=ONCE)


def of_layer(a, layer):
    return pl.BlockSpec((1,) + a.shape[1:], lambda i, p: (layer, 0, 0), pipeline_mode=ONCE)


def shape(*dims):
    return jax.ShapeDtypeStruct(dims, BF16)


def add(parts):
    return sum(p.astype(F32) for p in parts)


def spread(parts, axis):
    return [parts[0]] + [lax.ppermute(parts[d], axis, [(i, (i + d) % 4) for i in range(4)]) for d in (1, 2, 3)]


def chunk(a, index, rows):
    return lax.dynamic_slice_in_dim(a, index % 4 * rows, rows, 0)


def paired(w):
    return lax.ppermute(w, "x", [(0, 1), (1, 0), (2, 3), (3, 2)])


def crossed(w):
    return lax.ppermute(w, "x", [(1, 2), (2, 1)])


def body(acts, grads_out, weight_grad):
    y, x, z, c = (lax.axis_index(n) for n in ("y", "x", "z", "c"))
    pos = jnp.stack([x, y, c, z % 4 * 2 + c, z // 4, z]).astype(jnp.int32)
    rows, width = weight_grad.shape[1:]
    barrier = lax.optimization_barrier

    early, rest, mid = shape(rows - BLK, width), shape(BLK, width), shape(rows, 256)
    side, *own = call(
        side_kernel, pos, (acts, weight_grad),
        [pl.BlockSpec((1, acts.shape[1], 3 * BLK), lambda i, p: (p[4], 0, i)), ANYWHERE],
        [shape(128, LANES), early, mid],
        [VMEM(early.shape, BF16), VMEM(mid.shape, BF16), pltpu.SemaphoreType.DMA((2, 2))],
        out_specs=[pl.BlockSpec((32, LANES), lambda i, p: (i, 0)), ANYWHERE, ANYWHERE], vmem=60, grid=4,
    )
    pair0, mid0 = paired(own[0]), crossed(own[1])
    side, grads_out = barrier((side, grads_out))
    side = lax.all_to_all(side, "y", 0, 0, tiled=True)

    covs = call(
        cov_kernel, pos, (grads_out,), [whole(grads_out)], [shape(128, LANES)] * 4,
        [VMEM((2, 256, LANES), BF16)], vmem=60, flops=12_000_000_000,
    )
    start = covs[0]
    covs = spread(covs, "y")
    side, pair0, mid0 = barrier((side, pair0, mid0))
    side = call(total_kernel, pos, (side,), [whole(side)], [shape(128, LANES)], [], flops=60_000_000_000)[0]

    def sum_side(operands):
        pos, side, weight_grad, _ = operands
        side = lax.all_to_all(side, "x", 0, 0, tiled=True)
        late = [rest, shape(rows, width), mid]
        late = call(
            late_kernel, pos, (weight_grad,), [ANYWHERE], late,
            [VMEM(a.shape, BF16) for a in late] + [pltpu.SemaphoreType.DMA((2, 3))],
            out_specs=[ANYWHERE] * 3, vmem=60, flops=4_000_000_000,
        )
        return call(chosen_kernel, pos, (side,), [whole(side)], [shape(128, 2560)], [])[0], *late

    side, rest, pair1, mid1 = lax.cond(
        x + y + z + c < 64, sum_side,
        lambda operands: tuple(
            jnp.zeros(n, BF16) for n in ((128, 2560), rest.shape, (rows, width), mid.shape)
        ),
        (pos, side, weight_grad, start),
    )
    rest = paired(rest)
    mine = lax.all_to_all(side, "z", 0, 0, tiled=True)
    *covs, _, rest = barrier((*covs, side, rest))
    quarter = add(covs).astype(BF16)

    sends = [
        jnp.concatenate([chunk(quarter[:64], x + d, 16), chunk(quarter[64:], x + d, 16)], axis=0) for d in range(4)
    ]
    own = (add(spread(sends, "x")) * (1.0 / TOKENS)).astype(BF16)
    quarter = jnp.concatenate(spread([own] * 4, "x"), axis=0)
    quarter, pair1, mid1, mine = barrier((quarter, pair1, mid1, mine))
    pair1, mid1 = paired(pair1), crossed(mid1)
    parts = spread([quarter] * 4, "y")
    other = lax.ppermute(mine, "c", [(0, 1), (1, 0)])
    factor = call(
        factor_kernel, pos, (mine, other), [whole(mine), whole(other)], [shape(2, 1024, 384)],
        [VMEM((256, 2560), BF16), VMEM((2, 2, BLK, BLK), F32), VMEM((2, 1024, 1024), BF16)], flops=10_000_000_000,
    )[0]
    rights = [
        call(
            right_kernel, pos, (weight_grad, mid, factor, *pairs),
            [of_layer(weight_grad, layer), whole(mid), of_layer(factor, layer), *(whole(a) for a in pairs)],
            [shape(rows, width)], [],
        )[0]
        for layer, (mid, pairs) in enumerate(((mid0, (pair0, rest)), (mid1, (pair1,))))
    ]
    return call(
        left_kernel, pos, (*parts, *rights), [whole(a) for a in (*parts, *rights)],
        [shape(*weight_grad.shape)],
        [
            VMEM((2, 256, LANES), BF16), VMEM((2, 3, BLK, BLK), F32), VMEM((6, BLK, width), BF16),
            pltpu.SemaphoreType.DMA((6,)),
        ],
        out_specs=[ANYWHERE],
    )[0]


def solution(mesh):
    fine = Mesh(mesh.devices.reshape(4, 4, 8, 2), ("y", "x", "z", "c"))
    dp, owner = ("y", "x"), ("z", "c")
    in_specs = (P(None, dp, None), P(None, dp, owner), P(None, owner, dp))
    out_specs = P(None, owner, dp)
    return jax.shard_map(body, mesh=fine, in_specs=in_specs, out_specs=out_specs, check_vma=False)
```

```python
import functools

import jax
import jax.numpy as jnp
from jax import lax
from jax.experimental import pallas as pl
from jax.experimental.pallas import tpu as pltpu
from jax.sharding import Mesh, PartitionSpec as P

BLK = 512
SUB = 128
damping = 0.1
TOKENS = 4096
F32 = jnp.float32
BF16 = jnp.bfloat16
VMEM = pltpu.VMEM

PAIRS = [(r, c) for r in range(4) for c in range(r, 4)]
LANES = 15 * SUB
PARTS = 1024, 448, 64


def tn_dot(a, b):
    return lax.dot_general(a, b, (((0,), (0,)), ((), ())), preferred_element_type=F32)


def nn_dot(a, b):
    return lax.dot_general(a, b, (((1,), (0,)), ((), ())), preferred_element_type=F32)


def middle(pos):
    return pl.ds(pl.multiple_of(jnp.where(pos[0] == 1, SUB, 0), SUB), 256)


def late_kernel(pos, w, rest, out, mid, held_rest, held, held_mid, sems):
    last = PARTS[2]
    sources = (
        (w.at[0, pl.ds(w.shape[1] - last, last)], held_rest.at[pl.ds(0, last)], rest.at[pl.ds(0, last)]),
        (w.at[1, pl.ds(0, BLK)], held_rest.at[pl.ds(last, BLK)], rest.at[pl.ds(last, BLK)]),
        (w.at[1, pl.ds(BLK, out.shape[0])], held, out),
        (w.at[1, :, middle(pos)], held_mid, mid),
    )
    loads = [pltpu.make_async_copy(a, b, sems.at[0, n]) for n, (a, b, _) in enumerate(sources)]
    stores = [pltpu.make_async_copy(b, c, sems.at[1, n]) for n, (_, b, c) in enumerate(sources)]
    for load in loads:
        load.start()
    for load, store in zip(loads, stores):
        load.wait()
        store.start()
    for store in stores:
        store.wait()


def cov_kernel(pos, grads, h0, h1, h2, h3, pack):
    y = pos[1]
    for layer in range(2):
        for b in range(3):
            rows = grads[layer, :, b * BLK:(b + 1) * BLK]
            top = tn_dot(rows[:, :256], rows).astype(BF16)
            low = tn_dot(rows[:, 256:], rows[:, 256:]).astype(BF16)
            for i, (r, c) in enumerate(PAIRS):
                s = 10 * b + i
                if r < 2:
                    piece = top[r * SUB:(r + 1) * SUB, c * SUB:(c + 1) * SUB]
                else:
                    piece = low[(r - 2) * SUB:(r - 1) * SUB, (c - 2) * SUB:(c - 1) * SUB]
                pack[layer, s // 15 * SUB:(s // 15 + 1) * SUB, s % 15 * SUB:(s % 15 + 1) * SUB] = piece
    for d, send in enumerate((h0, h1, h2, h3)):
        at = pl.multiple_of((y + d) % 4 * 64, 64)
        send[0:64, :] = pack[0, pl.ds(at, 64), :]
        send[64:128, :] = pack[1, pl.ds(at, 64), :]


def side_kernel(pos, acts, w, out, early, following, mid, held, held_next, held_mid, sems):
    part, step = pos[3], pl.program_id(0)
    sources = (
        (w.at[0, pl.ds(0, PARTS[0])], held, early),
        (w.at[0, pl.ds(PARTS[0], PARTS[1])], held_next, following),
        (w.at[0, :, middle(pos)], held_mid, mid),
    )
    loads = [pltpu.make_async_copy(a, b, sems.at[0, n]) for n, (a, b, _) in enumerate(sources)]
    stores = [pltpu.make_async_copy(b, c, sems.at[1, n]) for n, (_, b, c) in enumerate(sources)]

    @pl.when(step == 0)
    def _():
        for load in loads:
            load.start()

    @pl.when(step == 2)
    def _():
        for load, store in zip(loads, stores):
            load.wait()
            store.start()

    k = lax.broadcasted_iota(jnp.int32, (BLK, 64), 0)
    m = lax.broadcasted_iota(jnp.int32, (BLK, 64), 1)
    select = jnp.where(k == m // 16 * SUB + part * 16 + m % 16, 1.0, 0.0).astype(BF16)
    for b in range(3):
        rows = acts[0, :, b * BLK:(b + 1) * BLK]
        chosen = nn_dot(rows, select).astype(BF16)
        cov = tn_dot(chosen, rows).astype(BF16)
        for i, (r, c) in enumerate(PAIRS):
            s = 10 * b + i
            at = s // 15 * 16
            out[at:at + 16, s % 15 * SUB:(s % 15 + 1) * SUB] = cov[r * 16:(r + 1) * 16, c * SUB:(c + 1) * SUB]

    @pl.when(step == 3)
    def _():
        for store in stores:
            store.wait()


def total_kernel(pos, parts, out):
    total = (parts[0:32, :].astype(F32) + parts[32:64, :].astype(F32)) + (
        parts[64:96, :].astype(F32) + parts[96:128, :].astype(F32)
    )
    for n in range(4):
        out[32 * n:32 * n + 32, :] = total.astype(BF16)


def chosen_kernel(pos, parts, out):
    x = pos[0]
    total = ((parts[0:32, :].astype(F32) + parts[32:64, :].astype(F32)) + (
        parts[64:96, :].astype(F32) + parts[96:128, :].astype(F32)
    )) * (1.0 / TOKENS)
    upper, lower = total[0:16, :].astype(BF16), total[16:32, :].astype(BF16)

    @pl.when(x < 2)
    def _():
        for n in range(8):
            out[16 * n:16 * n + 16, 0:LANES] = upper
            out[16 * n:16 * n + 16, LANES:2560] = lower[:, 0:640]

    @pl.when(x >= 2)
    def _():
        for n in range(8):
            out[16 * n:16 * n + 16, 0:640] = upper[:, 1280:LANES]
            out[16 * n:16 * n + 16, 640:2560] = lower


def unpack(piece, full):
    for i, (r, c) in enumerate(PAIRS):
        tile = piece(i)
        full[r * SUB:(r + 1) * SUB, c * SUB:(c + 1) * SUB] = tile.astype(full.dtype)
        if r != c:
            full[c * SUB:(c + 1) * SUB, r * SUB:(r + 1) * SUB] = tile.T.astype(full.dtype)


def invert(full):
    ri = lax.broadcasted_iota(jnp.int32, (BLK, BLK), 0)
    ci = lax.broadcasted_iota(jnp.int32, (BLK, BLK), 1)
    diagonal = ri == ci
    matrix = full[...] + jnp.where(diagonal, damping, 0.0)
    two_eye = jnp.where(diagonal, 2.0, 0.0)
    sums = jnp.sum(jnp.abs(matrix), axis=0, keepdims=True)
    alpha = (1.0 / jnp.max(sums, axis=1, keepdims=True)).astype(BF16).astype(F32)
    low = matrix.astype(BF16)
    residue = (two_eye - low.astype(F32) * alpha).astype(BF16)
    iterate = (residue.astype(F32) * alpha).astype(BF16)
    image = nn_dot(low, iterate)
    residue = (two_eye - image).astype(BF16)
    return nn_dot(iterate, residue).astype(BF16)


def factor_kernel(pos, mine, other, out, pack, full, diag):
    x, core = pos[0], pos[2]
    for z in range(8):
        rows = slice(16 * z, 16 * z + 16)
        pack[pl.ds(pl.multiple_of(32 * z + core * 16, 16), 16), :] = mine[rows, :]
        pack[pl.ds(pl.multiple_of(32 * z + 16 - core * 16, 16), 16), :] = other[rows, :]
    base = x // 2 * BLK
    own = pl.multiple_of(x * 384 - base, SUB)
    pair = pl.multiple_of((x + 1 - 2 * (x % 2)) * 384 - base, SUB)
    mid = pl.multiple_of(jnp.where(x == 1, 768, 0), SUB)
    columns = pl.ds(own, 384)
    for layer in range(2):
        for b in range(2):
            at = b * BLK
            unpack(
                lambda i: pack[layer * SUB:(layer + 1) * SUB, b * 1280 + i * SUB:b * 1280 + (i + 1) * SUB].astype(F32),
                full.at[layer, b],
            )
            diag[layer, at:at + BLK, at:at + BLK] = invert(full.at[layer, b])
            diag[layer, at:at + BLK, BLK - at:2 * BLK - at] = jnp.zeros((BLK, BLK), BF16)
        out[layer, 0:384, :] = diag[layer, pl.ds(own, 384), columns]
        out[layer, 384:768, :] = diag[layer, pl.ds(pair, 384), columns]
        out[layer, 768:1024, :] = diag[layer, pl.ds(mid, 256), columns]


def right_kernel(parts, pos, w_own, w_mid, factor, *refs):
    out, at = refs[-1], 0
    for pair, (first, count) in zip(refs[:-1], parts):
        rows = slice(at, at + count)
        total = nn_dot(w_own[0, rows, :], factor[0, 0:384, :])
        total += nn_dot(pair[first:first + count, :], factor[0, 384:768, :])
        total += nn_dot(w_mid[rows, :], factor[0, 768:1024, :])
        out[rows, :] = total.astype(BF16)
        at += count


def left_kernel(pos, p0, p1, p2, p3, r0, r1, out, pack, full, ready, sems):
    x, y = pos[0], pos[1]
    copies = []
    for layer, right in enumerate((r0, r1)):
        for d, part in enumerate((p0, p1, p2, p3)):
            for e in range(4):
                at = (y + 4 - d) % 4 * 64 + (x + 4 - e) % 4 * 16
                rows = 32 * e + 16 * layer
                pack[layer, pl.ds(pl.multiple_of(at, 16), 16), :] = part[rows:rows + 16, :]
        for b in range(3):
            def piece(i):
                s = 10 * b + i
                return pack[layer, s // 15 * SUB:(s // 15 + 1) * SUB, s % 15 * SUB:(s % 15 + 1) * SUB].astype(F32)

            unpack(piece, full.at[layer, b])
            at = b * BLK
            n = 3 * layer + b
            ready[n] = nn_dot(invert(full.at[layer, b]), right[at:at + BLK, :]).astype(BF16)
            copies.append(pltpu.make_async_copy(ready.at[n], out.at[layer, pl.ds(at, BLK)], sems.at[n]))
            copies[-1].start()
    for copy in copies:
        copy.wait()


def call(kernel, pos, operands, in_specs, out_shape, scratch, out_specs=None, vmem=40, flops=0, grid=1):
    return pl.pallas_call(
        kernel,
        grid_spec=pltpu.PrefetchScalarGridSpec(
            num_scalar_prefetch=1,
            grid=(grid,),
            in_specs=in_specs,
            out_specs=out_specs or [whole(s) for s in out_shape],
            scratch_shapes=scratch,
        ),
        out_shape=out_shape,
        compiler_params=pltpu.CompilerParams(vmem_limit_bytes=vmem * 1024 * 1024),
        cost_estimate=pl.CostEstimate(flops=flops, bytes_accessed=0, transcendentals=0),
    )(pos, *operands)


ANYWHERE = pl.BlockSpec(memory_space=pl.ANY)
ONCE = pl.Buffered(1)


def whole(a):
    return pl.BlockSpec(a.shape, lambda i, p, n=len(a.shape): (0,) * n, pipeline_mode=ONCE)


def of_layer(a, layer):
    return pl.BlockSpec((1,) + a.shape[1:], lambda i, p: (layer, 0, 0), pipeline_mode=ONCE)


def shape(*dims):
    return jax.ShapeDtypeStruct(dims, BF16)


def add(parts):
    return sum(p.astype(F32) for p in parts)


def spread(parts, axis):
    return [parts[0]] + [lax.ppermute(parts[d], axis, [(i, (i + d) % 4) for i in range(4)]) for d in (1, 2, 3)]


def chunk(a, index, rows):
    return lax.dynamic_slice_in_dim(a, index % 4 * rows, rows, 0)


def paired(w):
    return lax.ppermute(w, "x", [(0, 1), (1, 0), (2, 3), (3, 2)])


def crossed(w):
    return lax.ppermute(w, "x", [(1, 2), (2, 1)])


def body(acts, grads_out, weight_grad):
    y, x, z, c = (lax.axis_index(n) for n in ("y", "x", "z", "c"))
    pos = jnp.stack([x, y, c, z % 4 * 2 + c, z // 4, z]).astype(jnp.int32)
    rows, width = weight_grad.shape[1:]
    barrier = lax.optimization_barrier

    early, following, mid = shape(PARTS[0], width), shape(PARTS[1], width), shape(rows, 256)
    rest, late = shape(PARTS[2] + BLK, width), shape(rows - BLK, width)
    side, *own = call(
        side_kernel, pos, (acts, weight_grad),
        [pl.BlockSpec((1, acts.shape[1], 3 * BLK), lambda i, p: (p[4], 0, i)), ANYWHERE],
        [shape(128, LANES), early, following, mid],
        [VMEM(a.shape, BF16) for a in (early, following, mid)] + [pltpu.SemaphoreType.DMA((2, 3))],
        out_specs=[pl.BlockSpec((32, LANES), lambda i, p: (i, 0))] + [ANYWHERE] * 3, vmem=60, grid=4,
    )
    early, following, mid0 = paired(own[0]), paired(own[1]), crossed(own[2])
    side, grads_out = barrier((side, grads_out))
    side = lax.all_to_all(side, "y", 0, 0, tiled=True)

    covs = call(
        cov_kernel, pos, (grads_out,), [whole(grads_out)], [shape(128, LANES)] * 4,
        [VMEM((2, 256, LANES), BF16)], vmem=60, flops=12_000_000_000,
    )
    start = covs[0]
    covs = spread(covs, "y")
    side, early, mid0 = barrier((side, early, mid0))
    side = call(total_kernel, pos, (side,), [whole(side)], [shape(128, LANES)], [], flops=60_000_000_000)[0]

    def sum_side(operands):
        pos, side, weight_grad, _ = operands
        side = lax.all_to_all(side, "x", 0, 0, tiled=True)
        outs = [rest, late, mid]
        outs = call(
            late_kernel, pos, (weight_grad,), [ANYWHERE], outs,
            [VMEM(a.shape, BF16) for a in outs] + [pltpu.SemaphoreType.DMA((2, 4))],
            out_specs=[ANYWHERE] * 3, vmem=60, flops=4_000_000_000,
        )
        return call(chosen_kernel, pos, (side,), [whole(side)], [shape(128, 2560)], [])[0], *outs

    side, rest, late, mid1 = lax.cond(
        x + y + z + c < 64, sum_side,
        lambda operands: tuple(
            jnp.zeros(n, BF16) for n in ((128, 2560), rest.shape, late.shape, mid.shape)
        ),
        (pos, side, weight_grad, start),
    )
    side, rest, following = barrier((side, rest, following))
    rest = paired(rest)
    mine = lax.all_to_all(side, "z", 0, 0, tiled=True)
    *covs, _, rest = barrier((*covs, side, rest))
    quarter = add(covs).astype(BF16)

    sends = [
        jnp.concatenate([chunk(quarter[:64], x + d, 16), chunk(quarter[64:], x + d, 16)], axis=0) for d in range(4)
    ]
    own = (add(spread(sends, "x")) * (1.0 / TOKENS)).astype(BF16)
    quarter = jnp.concatenate(spread([own] * 4, "x"), axis=0)
    quarter, late, mid1, mine = barrier((quarter, late, mid1, mine))
    late, mid1 = paired(late), crossed(mid1)
    parts = spread([quarter] * 4, "y")
    other = lax.ppermute(mine, "c", [(0, 1), (1, 0)])
    factor = call(
        factor_kernel, pos, (mine, other), [whole(mine), whole(other)], [shape(2, 1024, 384)],
        [VMEM((256, 2560), BF16), VMEM((2, 2, BLK, BLK), F32), VMEM((2, 1024, 1024), BF16)], flops=10_000_000_000,
    )[0]
    rights = [
        call(
            functools.partial(right_kernel, parts_of), pos, (weight_grad, mid, factor, *pairs),
            [of_layer(weight_grad, layer), whole(mid), of_layer(factor, layer), *(whole(a) for a in pairs)],
            [shape(rows, width)], [],
        )[0]
        for layer, (mid, pairs, parts_of) in enumerate((
            (mid0, (early, following, rest), ((0, PARTS[0]), (0, PARTS[1]), (0, PARTS[2]))),
            (mid1, (rest, late), ((PARTS[2], BLK), (0, rows - BLK))),
        ))
    ]
    return call(
        left_kernel, pos, (*parts, *rights), [whole(a) for a in (*parts, *rights)],
        [shape(*weight_grad.shape)],
        [
            VMEM((2, 256, LANES), BF16), VMEM((2, 3, BLK, BLK), F32), VMEM((6, BLK, width), BF16),
            pltpu.SemaphoreType.DMA((6,)),
        ],
        out_specs=[ANYWHERE],
    )[0]


def solution(mesh):
    fine = Mesh(mesh.devices.reshape(4, 4, 8, 2), ("y", "x", "z", "c"))
    dp, owner = ("y", "x"), ("z", "c")
    in_specs = (P(None, dp, None), P(None, dp, owner), P(None, owner, dp))
    out_specs = P(None, owner, dp)
    return jax.shard_map(body, mesh=fine, in_specs=in_specs, out_specs=out_specs, check_vma=False)
```

```python
import functools

import jax
import jax.numpy as jnp
from jax import lax
from jax.experimental import pallas as pl
from jax.experimental.pallas import tpu as pltpu
from jax.sharding import Mesh, PartitionSpec as P

BLK = 512
SUB = 128
damping = 0.1
TOKENS = 4096
F32 = jnp.float32
BF16 = jnp.bfloat16
VMEM = pltpu.VMEM

PAIRS = [(r, c) for r in range(4) for c in range(r, 4)]
LANES = 15 * SUB
ABOVE = [(r, c) for r in range(4) for c in range(r + 1, 4)]
DENSE = 13 * SUB
PARTS = 1024, 496, 16


def tn_dot(a, b):
    return lax.dot_general(a, b, (((0,), (0,)), ((), ())), preferred_element_type=F32)


def nn_dot(a, b):
    return lax.dot_general(a, b, (((1,), (0,)), ((), ())), preferred_element_type=F32)


def middle(pos):
    return pl.ds(pl.multiple_of(jnp.where(pos[0] == 1, SUB, 0), SUB), 256)


def late_kernel(pos, w, rest, out, mid, held_rest, held, held_mid, sems):
    last = PARTS[2]
    sources = (
        (w.at[0, pl.ds(w.shape[1] - last, last)], held_rest.at[pl.ds(0, last)], rest.at[pl.ds(0, last)]),
        (w.at[1, pl.ds(0, BLK)], held_rest.at[pl.ds(last, BLK)], rest.at[pl.ds(last, BLK)]),
        (w.at[1, pl.ds(BLK, out.shape[0])], held, out),
        (w.at[1, :, middle(pos)], held_mid, mid),
    )
    loads = [pltpu.make_async_copy(a, b, sems.at[0, n]) for n, (a, b, _) in enumerate(sources)]
    stores = [pltpu.make_async_copy(b, c, sems.at[1, n]) for n, (_, b, c) in enumerate(sources)]
    for load in loads:
        load.start()
    for load, store in zip(loads, stores):
        load.wait()
        store.start()
    for store in stores:
        store.wait()


def cov_kernel(pos, grads, h0, h1, h2, h3, pack):
    y = pos[1]
    row = lax.broadcasted_iota(jnp.int32, (SUB, SUB), 0)
    column = lax.broadcasted_iota(jnp.int32, (SUB, SUB), 1)
    for layer in range(2):
        def store(s, tile):
            at = slice(s // 13 * SUB, (s // 13 + 1) * SUB), slice(s % 13 * SUB, (s % 13 + 1) * SUB)
            pack[layer, at[0], at[1]] = tile.astype(BF16)

        diagonals = jnp.zeros((SUB, SUB), F32)
        for b in range(3):
            rows = grads[layer, :, b * BLK:(b + 1) * BLK]
            halves = tn_dot(rows[:, :256], rows), tn_dot(rows[:, 256:], rows[:, 256:])

            def tile(r, c):
                first = r // 2 * 2
                return halves[r // 2][(r - first) * SUB:(r - first + 1) * SUB, (c - first) * SUB:(c - first + 1) * SUB]

            for i, (r, c) in enumerate(ABOVE):
                store(8 * b + i, tile(r, c))
            for k in range(2):
                lower = tile(2 * k + 1, 2 * k + 1)
                store(8 * b + 6 + k, jnp.where(row <= column, tile(2 * k, 2 * k), lower))
                line = jnp.sum(jnp.where(row == column, lower, 0.0), axis=1, keepdims=True)
                diagonals = jnp.where(column == 2 * b + k, line, diagonals)
        store(24, diagonals)
        store(25, jnp.zeros((SUB, SUB), F32))
    for d, send in enumerate((h0, h1, h2, h3)):
        at = pl.multiple_of((y + d) % 4 * 64, 64)
        send[0:64, :] = pack[0, pl.ds(at, 64), :]
        send[64:128, :] = pack[1, pl.ds(at, 64), :]


def side_kernel(pos, acts, w, out, early, following, mid, held, held_next, held_mid, sems):
    part, step = pos[3], pl.program_id(0)
    sources = (
        (w.at[0, pl.ds(0, PARTS[0])], held, early),
        (w.at[0, pl.ds(PARTS[0], PARTS[1])], held_next, following),
        (w.at[0, :, middle(pos)], held_mid, mid),
    )
    loads = [pltpu.make_async_copy(a, b, sems.at[0, n]) for n, (a, b, _) in enumerate(sources)]
    stores = [pltpu.make_async_copy(b, c, sems.at[1, n]) for n, (_, b, c) in enumerate(sources)]

    @pl.when(step == 0)
    def _():
        for load in loads:
            load.start()

    @pl.when(step == 2)
    def _():
        for load, store in zip(loads, stores):
            load.wait()
            store.start()

    k = lax.broadcasted_iota(jnp.int32, (BLK, 64), 0)
    m = lax.broadcasted_iota(jnp.int32, (BLK, 64), 1)
    select = jnp.where(k == m // 16 * SUB + part * 16 + m % 16, 1.0, 0.0).astype(BF16)
    for b in range(3):
        rows = acts[0, :, b * BLK:(b + 1) * BLK]
        chosen = nn_dot(rows, select).astype(BF16)
        cov = tn_dot(chosen, rows).astype(BF16)
        for i, (r, c) in enumerate(PAIRS):
            s = 10 * b + i
            at = s // 15 * 16
            out[at:at + 16, s % 15 * SUB:(s % 15 + 1) * SUB] = cov[r * 16:(r + 1) * 16, c * SUB:(c + 1) * SUB]

    @pl.when(step == 3)
    def _():
        for store in stores:
            store.wait()


def total_kernel(pos, parts, out):
    total = (parts[0:32, :].astype(F32) + parts[32:64, :].astype(F32)) + (
        parts[64:96, :].astype(F32) + parts[96:128, :].astype(F32)
    )
    for n in range(4):
        out[32 * n:32 * n + 32, :] = total.astype(BF16)


def chosen_kernel(pos, parts, out):
    x = pos[0]
    total = ((parts[0:32, :].astype(F32) + parts[32:64, :].astype(F32)) + (
        parts[64:96, :].astype(F32) + parts[96:128, :].astype(F32)
    )) * (1.0 / TOKENS)
    upper, lower = total[0:16, :].astype(BF16), total[16:32, :].astype(BF16)

    @pl.when(x < 2)
    def _():
        for n in range(8):
            out[16 * n:16 * n + 16, 0:LANES] = upper
            out[16 * n:16 * n + 16, LANES:2560] = lower[:, 0:640]

    @pl.when(x >= 2)
    def _():
        for n in range(8):
            out[16 * n:16 * n + 16, 0:640] = upper[:, 1280:LANES]
            out[16 * n:16 * n + 16, 640:2560] = lower


def unpack(piece, full):
    for i, (r, c) in enumerate(PAIRS):
        tile = piece(i)
        full[r * SUB:(r + 1) * SUB, c * SUB:(c + 1) * SUB] = tile.astype(full.dtype)
        if r != c:
            full[c * SUB:(c + 1) * SUB, r * SUB:(r + 1) * SUB] = tile.T.astype(full.dtype)


def unpack_dense(b, tile, full):
    row = lax.broadcasted_iota(jnp.int32, (SUB, SUB), 0)
    column = lax.broadcasted_iota(jnp.int32, (SUB, SUB), 1)
    at = [slice(n * SUB, (n + 1) * SUB) for n in range(4)]
    for i, (r, c) in enumerate(ABOVE):
        piece = tile(8 * b + i)
        full[at[r], at[c]] = piece
        full[at[c], at[r]] = piece.T
    diagonals = tile(24)
    for k in range(2):
        piece = tile(8 * b + 6 + k)
        turned = piece.T
        line = jnp.sum(jnp.where(column == 2 * b + k, diagonals, 0.0), axis=1, keepdims=True)
        full[at[2 * k], at[2 * k]] = jnp.where(row <= column, piece, turned)
        full[at[2 * k + 1], at[2 * k + 1]] = jnp.where(row > column, piece, jnp.where(row == column, line, turned))


def invert(full):
    ri = lax.broadcasted_iota(jnp.int32, (BLK, BLK), 0)
    ci = lax.broadcasted_iota(jnp.int32, (BLK, BLK), 1)
    diagonal = ri == ci
    matrix = full[...] + jnp.where(diagonal, damping, 0.0)
    two_eye = jnp.where(diagonal, 2.0, 0.0)
    sums = jnp.sum(jnp.abs(matrix), axis=0, keepdims=True)
    alpha = (1.0 / jnp.max(sums, axis=1, keepdims=True)).astype(BF16).astype(F32)
    low = matrix.astype(BF16)
    residue = (two_eye - low.astype(F32) * alpha).astype(BF16)
    iterate = (residue.astype(F32) * alpha).astype(BF16)
    image = nn_dot(low, iterate)
    residue = (two_eye - image).astype(BF16)
    return nn_dot(iterate, residue).astype(BF16)


def factor_kernel(pos, mine, other, out, pack, full, diag):
    x, core = pos[0], pos[2]
    for z in range(8):
        rows = slice(16 * z, 16 * z + 16)
        pack[pl.ds(pl.multiple_of(32 * z + core * 16, 16), 16), :] = mine[rows, :]
        pack[pl.ds(pl.multiple_of(32 * z + 16 - core * 16, 16), 16), :] = other[rows, :]
    base = x // 2 * BLK
    own = pl.multiple_of(x * 384 - base, SUB)
    pair = pl.multiple_of((x + 1 - 2 * (x % 2)) * 384 - base, SUB)
    mid = pl.multiple_of(jnp.where(x == 1, 768, 0), SUB)
    columns = pl.ds(own, 384)
    for layer in range(2):
        for b in range(2):
            at = b * BLK
            unpack(
                lambda i: pack[layer * SUB:(layer + 1) * SUB, b * 1280 + i * SUB:b * 1280 + (i + 1) * SUB].astype(F32),
                full.at[layer, b],
            )
            diag[layer, at:at + BLK, at:at + BLK] = invert(full.at[layer, b])
            diag[layer, at:at + BLK, BLK - at:2 * BLK - at] = jnp.zeros((BLK, BLK), BF16)
        out[layer, 0:384, :] = diag[layer, pl.ds(own, 384), columns]
        out[layer, 384:768, :] = diag[layer, pl.ds(pair, 384), columns]
        out[layer, 768:1024, :] = diag[layer, pl.ds(mid, 256), columns]


def right_kernel(parts, pos, w_own, w_mid, factor, *refs):
    out, at = refs[-1], 0
    for pair, (first, count) in zip(refs[:-1], parts):
        rows = slice(at, at + count)
        total = nn_dot(w_own[0, rows, :], factor[0, 0:384, :])
        total += nn_dot(pair[first:first + count, :], factor[0, 384:768, :])
        total += nn_dot(w_mid[rows, :], factor[0, 768:1024, :])
        out[rows, :] = total.astype(BF16)
        at += count


def left_kernel(pos, p0, p1, p2, p3, r0, r1, out, pack, full, ready, sems):
    x, y = pos[0], pos[1]
    copies = []
    for layer, right in enumerate((r0, r1)):
        for d, part in enumerate((p0, p1, p2, p3)):
            for e in range(4):
                at = (y + 4 - d) % 4 * 64 + (x + 4 - e) % 4 * 16
                rows = 32 * e + 16 * layer
                pack[layer, pl.ds(pl.multiple_of(at, 16), 16), :] = part[rows:rows + 16, :]
        def tile(s):
            return pack[layer, s // 13 * SUB:(s // 13 + 1) * SUB, s % 13 * SUB:(s % 13 + 1) * SUB].astype(F32)

        for b in range(3):
            unpack_dense(b, tile, full.at[layer, b])
            at = b * BLK
            n = 3 * layer + b
            ready[n] = nn_dot(invert(full.at[layer, b]), right[at:at + BLK, :]).astype(BF16)
            copies.append(pltpu.make_async_copy(ready.at[n], out.at[layer, pl.ds(at, BLK)], sems.at[n]))
            copies[-1].start()
    for copy in copies:
        copy.wait()


def call(kernel, pos, operands, in_specs, out_shape, scratch, out_specs=None, vmem=40, flops=0, grid=1):
    return pl.pallas_call(
        kernel,
        grid_spec=pltpu.PrefetchScalarGridSpec(
            num_scalar_prefetch=1,
            grid=(grid,),
            in_specs=in_specs,
            out_specs=out_specs or [whole(s) for s in out_shape],
            scratch_shapes=scratch,
        ),
        out_shape=out_shape,
        compiler_params=pltpu.CompilerParams(vmem_limit_bytes=vmem * 1024 * 1024),
        cost_estimate=pl.CostEstimate(flops=flops, bytes_accessed=0, transcendentals=0),
    )(pos, *operands)


ANYWHERE = pl.BlockSpec(memory_space=pl.ANY)
ONCE = pl.Buffered(1)


def whole(a):
    return pl.BlockSpec(a.shape, lambda i, p, n=len(a.shape): (0,) * n, pipeline_mode=ONCE)


def of_layer(a, layer):
    return pl.BlockSpec((1,) + a.shape[1:], lambda i, p: (layer, 0, 0), pipeline_mode=ONCE)


def shape(*dims):
    return jax.ShapeDtypeStruct(dims, BF16)


def add(parts):
    return sum(p.astype(F32) for p in parts)


def spread(parts, axis):
    return [parts[0]] + [lax.ppermute(parts[d], axis, [(i, (i + d) % 4) for i in range(4)]) for d in (1, 2, 3)]


def chunk(a, index, rows):
    return lax.dynamic_slice_in_dim(a, index % 4 * rows, rows, 0)


def paired(w):
    return lax.ppermute(w, "x", [(0, 1), (1, 0), (2, 3), (3, 2)])


def crossed(w):
    return lax.ppermute(w, "x", [(1, 2), (2, 1)])


def body(acts, grads_out, weight_grad):
    y, x, z, c = (lax.axis_index(n) for n in ("y", "x", "z", "c"))
    pos = jnp.stack([x, y, c, z % 4 * 2 + c, z // 4, z]).astype(jnp.int32)
    rows, width = weight_grad.shape[1:]
    barrier = lax.optimization_barrier

    early, following, mid = shape(PARTS[0], width), shape(PARTS[1], width), shape(rows, 256)
    rest, late = shape(PARTS[2] + BLK, width), shape(rows - BLK, width)
    side, *own = call(
        side_kernel, pos, (acts, weight_grad),
        [pl.BlockSpec((1, acts.shape[1], 3 * BLK), lambda i, p: (p[4], 0, i)), ANYWHERE],
        [shape(128, LANES), early, following, mid],
        [VMEM(a.shape, BF16) for a in (early, following, mid)] + [pltpu.SemaphoreType.DMA((2, 3))],
        out_specs=[pl.BlockSpec((32, LANES), lambda i, p: (i, 0))] + [ANYWHERE] * 3, vmem=60, grid=4,
    )
    early, following, mid0 = paired(own[0]), paired(own[1]), crossed(own[2])
    side, grads_out = barrier((side, grads_out))
    side = lax.all_to_all(side, "y", 0, 0, tiled=True)

    covs = call(
        cov_kernel, pos, (grads_out,), [whole(grads_out)], [shape(128, DENSE)] * 4,
        [VMEM((2, 256, DENSE), BF16)], vmem=60, flops=12_000_000_000,
    )
    start = covs[0]
    covs = spread(covs, "y")
    side, early, mid0 = barrier((side, early, mid0))
    side = call(total_kernel, pos, (side,), [whole(side)], [shape(128, LANES)], [], flops=60_000_000_000)[0]

    def sum_side(operands):
        pos, side, weight_grad, _ = operands
        side = lax.all_to_all(side, "x", 0, 0, tiled=True)
        outs = [rest, late, mid]
        outs = call(
            late_kernel, pos, (weight_grad,), [ANYWHERE], outs,
            [VMEM(a.shape, BF16) for a in outs] + [pltpu.SemaphoreType.DMA((2, 4))],
            out_specs=[ANYWHERE] * 3, vmem=60, flops=4_000_000_000,
        )
        return call(chosen_kernel, pos, (side,), [whole(side)], [shape(128, 2560)], [])[0], *outs

    side, rest, late, mid1 = lax.cond(
        x + y + z + c < 64, sum_side,
        lambda operands: tuple(
            jnp.zeros(n, BF16) for n in ((128, 2560), rest.shape, late.shape, mid.shape)
        ),
        (pos, side, weight_grad, start),
    )
    side, rest, following = barrier((side, rest, following))
    rest = paired(rest)
    mine = lax.all_to_all(side, "z", 0, 0, tiled=True)
    *covs, _, rest = barrier((*covs, side, rest))
    quarter = add(covs).astype(BF16)

    sends = [
        jnp.concatenate([chunk(quarter[:64], x + d, 16), chunk(quarter[64:], x + d, 16)], axis=0) for d in range(4)
    ]
    own = (add(spread(sends, "x")) * (1.0 / TOKENS)).astype(BF16)
    quarter = jnp.concatenate(spread([own] * 4, "x"), axis=0)
    quarter, late, mid1, mine = barrier((quarter, late, mid1, mine))
    late, mid1 = paired(late), crossed(mid1)
    parts = spread([quarter] * 4, "y")
    other = lax.ppermute(mine, "c", [(0, 1), (1, 0)])
    factor = call(
        factor_kernel, pos, (mine, other), [whole(mine), whole(other)], [shape(2, 1024, 384)],
        [VMEM((256, 2560), BF16), VMEM((2, 2, BLK, BLK), F32), VMEM((2, 1024, 1024), BF16)], flops=10_000_000_000,
    )[0]
    rights = [
        call(
            functools.partial(right_kernel, parts_of), pos, (weight_grad, mid, factor, *pairs),
            [of_layer(weight_grad, layer), whole(mid), of_layer(factor, layer), *(whole(a) for a in pairs)],
            [shape(rows, width)], [],
        )[0]
        for layer, (mid, pairs, parts_of) in enumerate((
            (mid0, (early, following, rest), ((0, PARTS[0]), (0, PARTS[1]), (0, PARTS[2]))),
            (mid1, (rest, late), ((PARTS[2], BLK), (0, rows - BLK))),
        ))
    ]
    return call(
        left_kernel, pos, (*parts, *rights), [whole(a) for a in (*parts, *rights)],
        [shape(*weight_grad.shape)],
        [
            VMEM((2, 256, DENSE), BF16), VMEM((2, 3, BLK, BLK), F32), VMEM((6, BLK, width), BF16),
            pltpu.SemaphoreType.DMA((6,)),
        ],
        out_specs=[ANYWHERE],
    )[0]


def solution(mesh):
    fine = Mesh(mesh.devices.reshape(4, 4, 8, 2), ("y", "x", "z", "c"))
    dp, owner = ("y", "x"), ("z", "c")
    in_specs = (P(None, dp, None), P(None, dp, owner), P(None, owner, dp))
    out_specs = P(None, owner, dp)
    return jax.shard_map(body, mesh=fine, in_specs=in_specs, out_specs=out_specs, check_vma=False)
```

```python
import functools

import jax
import jax.numpy as jnp
from jax import lax
from jax.experimental import pallas as pl
from jax.experimental.pallas import tpu as pltpu
from jax.sharding import Mesh, PartitionSpec as P

BLK = 512
SUB = 128
damping = 0.1
TOKENS = 4096
F32 = jnp.float32
BF16 = jnp.bfloat16
VMEM = pltpu.VMEM

PAIRS = [(r, c) for r in range(4) for c in range(r, 4)]
LANES = 15 * SUB
ABOVE = [(r, c) for r in range(4) for c in range(r + 1, 4)]
DENSE = 13 * SUB
PARTS = 1024, (512, 96), 528, 912


def tn_dot(a, b):
    return lax.dot_general(a, b, (((0,), (0,)), ((), ())), preferred_element_type=F32)


def nn_dot(a, b):
    return lax.dot_general(a, b, (((1,), (0,)), ((), ())), preferred_element_type=F32)


def middle(pos):
    return pl.ds(pl.multiple_of(jnp.where(pos[0] == 1, SUB, 0), SUB), 256)


def late_kernel(pos, w, rest, out, mid, held_rest, held, held_mid, sems):
    first = PARTS[1][1]
    sources = (
        (w.at[1, pl.ds(first, PARTS[2])], held_rest, rest),
        (w.at[1, pl.ds(first + PARTS[2], PARTS[3])], held, out),
        (w.at[1, :, middle(pos)], held_mid, mid),
    )
    loads = [pltpu.make_async_copy(a, b, sems.at[0, n]) for n, (a, b, _) in enumerate(sources)]
    stores = [pltpu.make_async_copy(b, c, sems.at[1, n]) for n, (_, b, c) in enumerate(sources)]
    for load in loads:
        load.start()
    for load, store in zip(loads, stores):
        load.wait()
        store.start()
    for store in stores:
        store.wait()


def cov_kernel(pos, grads, h0, h1, h2, h3, pack):
    y = pos[1]
    row = lax.broadcasted_iota(jnp.int32, (SUB, SUB), 0)
    column = lax.broadcasted_iota(jnp.int32, (SUB, SUB), 1)
    for layer in range(2):
        def store(s, tile):
            at = slice(s // 13 * SUB, (s // 13 + 1) * SUB), slice(s % 13 * SUB, (s % 13 + 1) * SUB)
            pack[layer, at[0], at[1]] = tile.astype(BF16)

        diagonals = jnp.zeros((SUB, SUB), F32)
        for b in range(3):
            rows = grads[layer, :, b * BLK:(b + 1) * BLK]
            halves = tn_dot(rows[:, :256], rows), tn_dot(rows[:, 256:], rows[:, 256:])

            def tile(r, c):
                first = r // 2 * 2
                return halves[r // 2][(r - first) * SUB:(r - first + 1) * SUB, (c - first) * SUB:(c - first + 1) * SUB]

            for i, (r, c) in enumerate(ABOVE):
                store(8 * b + i, tile(r, c))
            for k in range(2):
                lower = tile(2 * k + 1, 2 * k + 1)
                store(8 * b + 6 + k, jnp.where(row <= column, tile(2 * k, 2 * k), lower))
                line = jnp.sum(jnp.where(row == column, lower, 0.0), axis=1, keepdims=True)
                diagonals = jnp.where(column == 2 * b + k, line, diagonals)
        store(24, diagonals)
        store(25, jnp.zeros((SUB, SUB), F32))
    for d, send in enumerate((h0, h1, h2, h3)):
        at = pl.multiple_of((y + d) % 4 * 64, 64)
        send[0:64, :] = pack[0, pl.ds(at, 64), :]
        send[64:128, :] = pack[1, pl.ds(at, 64), :]


def side_kernel(pos, acts, w, out, early, following, mid, held, held_next, held_mid, sems):
    part, step = pos[3], pl.program_id(0)
    upper, lower = PARTS[1]
    sources = (
        (w.at[0, pl.ds(0, PARTS[0])], held, early),
        (w.at[0, pl.ds(PARTS[0], upper)], held_next.at[pl.ds(0, upper)], following.at[pl.ds(0, upper)]),
        (w.at[1, pl.ds(0, lower)], held_next.at[pl.ds(upper, lower)], following.at[pl.ds(upper, lower)]),
        (w.at[0, :, middle(pos)], held_mid, mid),
    )
    loads = [pltpu.make_async_copy(a, b, sems.at[0, n]) for n, (a, b, _) in enumerate(sources)]
    stores = [pltpu.make_async_copy(b, c, sems.at[1, n]) for n, (_, b, c) in enumerate(sources)]

    @pl.when(step == 0)
    def _():
        for load in loads:
            load.start()

    @pl.when(step == 2)
    def _():
        for load, store in zip(loads, stores):
            load.wait()
            store.start()

    k = lax.broadcasted_iota(jnp.int32, (BLK, 64), 0)
    m = lax.broadcasted_iota(jnp.int32, (BLK, 64), 1)
    select = jnp.where(k == m // 16 * SUB + part * 16 + m % 16, 1.0, 0.0).astype(BF16)
    for b in range(3):
        rows = acts[0, :, b * BLK:(b + 1) * BLK]
        chosen = nn_dot(rows, select).astype(BF16)
        cov = tn_dot(chosen, rows).astype(BF16)
        for i, (r, c) in enumerate(PAIRS):
            s = 10 * b + i
            at = s // 15 * 16
            out[at:at + 16, s % 15 * SUB:(s % 15 + 1) * SUB] = cov[r * 16:(r + 1) * 16, c * SUB:(c + 1) * SUB]

    @pl.when(step == 3)
    def _():
        for store in stores:
            store.wait()


def total_kernel(pos, parts, out):
    total = (parts[0:32, :].astype(F32) + parts[32:64, :].astype(F32)) + (
        parts[64:96, :].astype(F32) + parts[96:128, :].astype(F32)
    )
    for n in range(4):
        out[32 * n:32 * n + 32, :] = total.astype(BF16)


def chosen_kernel(pos, parts, out):
    x = pos[0]
    total = ((parts[0:32, :].astype(F32) + parts[32:64, :].astype(F32)) + (
        parts[64:96, :].astype(F32) + parts[96:128, :].astype(F32)
    )) * (1.0 / TOKENS)
    upper, lower = total[0:16, :].astype(BF16), total[16:32, :].astype(BF16)

    @pl.when(x < 2)
    def _():
        for n in range(8):
            out[16 * n:16 * n + 16, 0:LANES] = upper
            out[16 * n:16 * n + 16, LANES:2560] = lower[:, 0:640]

    @pl.when(x >= 2)
    def _():
        for n in range(8):
            out[16 * n:16 * n + 16, 0:640] = upper[:, 1280:LANES]
            out[16 * n:16 * n + 16, 640:2560] = lower


def unpack(piece, full):
    for i, (r, c) in enumerate(PAIRS):
        tile = piece(i)
        full[r * SUB:(r + 1) * SUB, c * SUB:(c + 1) * SUB] = tile.astype(full.dtype)
        if r != c:
            full[c * SUB:(c + 1) * SUB, r * SUB:(r + 1) * SUB] = tile.T.astype(full.dtype)


def unpack_dense(b, tile, full):
    row = lax.broadcasted_iota(jnp.int32, (SUB, SUB), 0)
    column = lax.broadcasted_iota(jnp.int32, (SUB, SUB), 1)
    at = [slice(n * SUB, (n + 1) * SUB) for n in range(4)]
    for i, (r, c) in enumerate(ABOVE):
        piece = tile(8 * b + i)
        full[at[r], at[c]] = piece
        full[at[c], at[r]] = piece.T
    diagonals = tile(24)
    for k in range(2):
        piece = tile(8 * b + 6 + k)
        turned = piece.T
        line = jnp.sum(jnp.where(column == 2 * b + k, diagonals, 0.0), axis=1, keepdims=True)
        full[at[2 * k], at[2 * k]] = jnp.where(row <= column, piece, turned)
        full[at[2 * k + 1], at[2 * k + 1]] = jnp.where(row > column, piece, jnp.where(row == column, line, turned))


def invert(full):
    ri = lax.broadcasted_iota(jnp.int32, (BLK, BLK), 0)
    ci = lax.broadcasted_iota(jnp.int32, (BLK, BLK), 1)
    diagonal = ri == ci
    matrix = full[...] + jnp.where(diagonal, damping, 0.0)
    two_eye = jnp.where(diagonal, 2.0, 0.0)
    sums = jnp.sum(jnp.abs(matrix), axis=0, keepdims=True)
    alpha = (1.0 / jnp.max(sums, axis=1, keepdims=True)).astype(BF16).astype(F32)
    low = matrix.astype(BF16)
    residue = (two_eye - low.astype(F32) * alpha).astype(BF16)
    iterate = (residue.astype(F32) * alpha).astype(BF16)
    image = nn_dot(low, iterate)
    residue = (two_eye - image).astype(BF16)
    return nn_dot(iterate, residue).astype(BF16)


def factor_kernel(pos, mine, other, out, pack, full, diag):
    x, core = pos[0], pos[2]
    for z in range(8):
        rows = slice(16 * z, 16 * z + 16)
        pack[pl.ds(pl.multiple_of(32 * z + core * 16, 16), 16), :] = mine[rows, :]
        pack[pl.ds(pl.multiple_of(32 * z + 16 - core * 16, 16), 16), :] = other[rows, :]
    base = x // 2 * BLK
    own = pl.multiple_of(x * 384 - base, SUB)
    pair = pl.multiple_of((x + 1 - 2 * (x % 2)) * 384 - base, SUB)
    mid = pl.multiple_of(jnp.where(x == 1, 768, 0), SUB)
    columns = pl.ds(own, 384)
    for layer in range(2):
        for b in range(2):
            at = b * BLK
            unpack(
                lambda i: pack[layer * SUB:(layer + 1) * SUB, b * 1280 + i * SUB:b * 1280 + (i + 1) * SUB].astype(F32),
                full.at[layer, b],
            )
            diag[layer, at:at + BLK, at:at + BLK] = invert(full.at[layer, b])
            diag[layer, at:at + BLK, BLK - at:2 * BLK - at] = jnp.zeros((BLK, BLK), BF16)
        out[layer, 0:384, :] = diag[layer, pl.ds(own, 384), columns]
        out[layer, 384:768, :] = diag[layer, pl.ds(pair, 384), columns]
        out[layer, 768:1024, :] = diag[layer, pl.ds(mid, 256), columns]


def right_kernel(parts, pos, w_own, w_mid, factor, *refs):
    out, at = refs[-1], 0
    for pair, (first, count) in zip(refs[:-1], parts):
        rows = slice(at, at + count)
        total = nn_dot(w_own[0, rows, :], factor[0, 0:384, :])
        total += nn_dot(pair[first:first + count, :], factor[0, 384:768, :])
        total += nn_dot(w_mid[rows, :], factor[0, 768:1024, :])
        out[rows, :] = total.astype(BF16)
        at += count


def left_kernel(pos, p0, p1, p2, p3, r0, r1, out, pack, full, ready, sems):
    x, y = pos[0], pos[1]
    copies = []
    for layer, right in enumerate((r0, r1)):
        for d, part in enumerate((p0, p1, p2, p3)):
            for e in range(4):
                at = (y + 4 - d) % 4 * 64 + (x + 4 - e) % 4 * 16
                rows = 32 * e + 16 * layer
                pack[layer, pl.ds(pl.multiple_of(at, 16), 16), :] = part[rows:rows + 16, :]
        def tile(s):
            return pack[layer, s // 13 * SUB:(s // 13 + 1) * SUB, s % 13 * SUB:(s % 13 + 1) * SUB].astype(F32)

        for b in range(3):
            unpack_dense(b, tile, full.at[layer, b])
            at = b * BLK
            n = 3 * layer + b
            ready[n] = nn_dot(invert(full.at[layer, b]), right[at:at + BLK, :]).astype(BF16)
            copies.append(pltpu.make_async_copy(ready.at[n], out.at[layer, pl.ds(at, BLK)], sems.at[n]))
            copies[-1].start()
    for copy in copies:
        copy.wait()


def call(kernel, pos, operands, in_specs, out_shape, scratch, out_specs=None, vmem=40, flops=0, grid=1):
    return pl.pallas_call(
        kernel,
        grid_spec=pltpu.PrefetchScalarGridSpec(
            num_scalar_prefetch=1,
            grid=(grid,),
            in_specs=in_specs,
            out_specs=out_specs or [whole(s) for s in out_shape],
            scratch_shapes=scratch,
        ),
        out_shape=out_shape,
        compiler_params=pltpu.CompilerParams(vmem_limit_bytes=vmem * 1024 * 1024),
        cost_estimate=pl.CostEstimate(flops=flops, bytes_accessed=0, transcendentals=0),
    )(pos, *operands)


ANYWHERE = pl.BlockSpec(memory_space=pl.ANY)
ONCE = pl.Buffered(1)


def whole(a):
    return pl.BlockSpec(a.shape, lambda i, p, n=len(a.shape): (0,) * n, pipeline_mode=ONCE)


def of_layer(a, layer):
    return pl.BlockSpec((1,) + a.shape[1:], lambda i, p: (layer, 0, 0), pipeline_mode=ONCE)


def shape(*dims):
    return jax.ShapeDtypeStruct(dims, BF16)


def add(parts):
    return sum(p.astype(F32) for p in parts)


def spread(parts, axis):
    return [parts[0]] + [lax.ppermute(parts[d], axis, [(i, (i + d) % 4) for i in range(4)]) for d in (1, 2, 3)]


def chunk(a, index, rows):
    return lax.dynamic_slice_in_dim(a, index % 4 * rows, rows, 0)


def paired(w):
    return lax.ppermute(w, "x", [(0, 1), (1, 0), (2, 3), (3, 2)])


def crossed(w):
    return lax.ppermute(w, "x", [(1, 2), (2, 1)])


def body(acts, grads_out, weight_grad):
    y, x, z, c = (lax.axis_index(n) for n in ("y", "x", "z", "c"))
    pos = jnp.stack([x, y, c, z % 4 * 2 + c, z // 4, z]).astype(jnp.int32)
    rows, width = weight_grad.shape[1:]
    barrier = lax.optimization_barrier

    early, following, mid = shape(PARTS[0], width), shape(sum(PARTS[1]), width), shape(rows, 256)
    rest, late = shape(PARTS[2], width), shape(PARTS[3], width)
    side, *own = call(
        side_kernel, pos, (acts, weight_grad),
        [pl.BlockSpec((1, acts.shape[1], 3 * BLK), lambda i, p: (p[4], 0, i)), ANYWHERE],
        [shape(128, LANES), early, following, mid],
        [VMEM(a.shape, BF16) for a in (early, following, mid)] + [pltpu.SemaphoreType.DMA((2, 4))],
        out_specs=[pl.BlockSpec((32, LANES), lambda i, p: (i, 0))] + [ANYWHERE] * 3, vmem=60, grid=4,
    )
    early, following, mid0 = paired(own[0]), paired(own[1]), crossed(own[2])
    side, grads_out = barrier((side, grads_out))
    side = lax.all_to_all(side, "y", 0, 0, tiled=True)

    covs = call(
        cov_kernel, pos, (grads_out,), [whole(grads_out)], [shape(128, DENSE)] * 4,
        [VMEM((2, 256, DENSE), BF16)], vmem=60, flops=12_000_000_000,
    )
    start = covs[0]
    covs = spread(covs, "y")
    side, early, mid0 = barrier((side, early, mid0))
    side = call(total_kernel, pos, (side,), [whole(side)], [shape(128, LANES)], [], flops=60_000_000_000)[0]

    def sum_side(operands):
        pos, side, weight_grad, _ = operands
        side = lax.all_to_all(side, "x", 0, 0, tiled=True)
        outs = [rest, late, mid]
        outs = call(
            late_kernel, pos, (weight_grad,), [ANYWHERE], outs,
            [VMEM(a.shape, BF16) for a in outs] + [pltpu.SemaphoreType.DMA((2, 4))],
            out_specs=[ANYWHERE] * 3, vmem=60, flops=4_000_000_000,
        )
        return call(chosen_kernel, pos, (side,), [whole(side)], [shape(128, 2560)], [])[0], *outs

    side, rest, late, mid1 = lax.cond(
        x + y + z + c < 64, sum_side,
        lambda operands: tuple(
            jnp.zeros(n, BF16) for n in ((128, 2560), rest.shape, late.shape, mid.shape)
        ),
        (pos, side, weight_grad, start),
    )
    side, rest, following = barrier((side, rest, following))
    rest = paired(rest)
    mine = lax.all_to_all(side, "z", 0, 0, tiled=True)
    *covs, _, rest = barrier((*covs, side, rest))
    quarter = add(covs).astype(BF16)

    sends = [
        jnp.concatenate([chunk(quarter[:64], x + d, 16), chunk(quarter[64:], x + d, 16)], axis=0) for d in range(4)
    ]
    own = (add(spread(sends, "x")) * (1.0 / TOKENS)).astype(BF16)
    quarter = jnp.concatenate(spread([own] * 4, "x"), axis=0)
    quarter, late, mid1, mine = barrier((quarter, late, mid1, mine))
    late, mid1 = paired(late), crossed(mid1)
    parts = spread([quarter] * 4, "y")
    other = lax.ppermute(mine, "c", [(0, 1), (1, 0)])
    factor = call(
        factor_kernel, pos, (mine, other), [whole(mine), whole(other)], [shape(2, 1024, 384)],
        [VMEM((256, 2560), BF16), VMEM((2, 2, BLK, BLK), F32), VMEM((2, 1024, 1024), BF16)], flops=10_000_000_000,
    )[0]
    rights = [
        call(
            functools.partial(right_kernel, parts_of), pos, (weight_grad, mid, factor, *pairs),
            [of_layer(weight_grad, layer), whole(mid), of_layer(factor, layer), *(whole(a) for a in pairs)],
            [shape(rows, width)], [],
        )[0]
        for layer, (mid, pairs, parts_of) in enumerate((
            (mid0, (early, following), ((0, PARTS[0]), (0, PARTS[1][0]))),
            (mid1, (following, rest, late), (PARTS[1], (0, PARTS[2]), (0, PARTS[3]))),
        ))
    ]
    return call(
        left_kernel, pos, (*parts, *rights), [whole(a) for a in (*parts, *rights)],
        [shape(*weight_grad.shape)],
        [
            VMEM((2, 256, DENSE), BF16), VMEM((2, 3, BLK, BLK), F32), VMEM((6, BLK, width), BF16),
            pltpu.SemaphoreType.DMA((6,)),
        ],
        out_specs=[ANYWHERE],
    )[0]


def solution(mesh):
    fine = Mesh(mesh.devices.reshape(4, 4, 8, 2), ("y", "x", "z", "c"))
    dp, owner = ("y", "x"), ("z", "c")
    in_specs = (P(None, dp, None), P(None, dp, owner), P(None, owner, dp))
    out_specs = P(None, owner, dp)
    return jax.shard_map(body, mesh=fine, in_specs=in_specs, out_specs=out_specs, check_vma=False)
```
